32 devices in a mesh: slab: 2 (over x), col: 16 (over z, y, core).
Axes of the slice: x: 2, y: 2, z: 4, core: 2. Of those that a mesh axis runs over, the one named last changes fastest.
Arguments:
- tiles: bfloat16 [192, 12, 128, 128], P(('slab', 'col')), parts along dimension 0, may hold values from -6 to 6
- tile_cols: int32 [192, 12], P(('slab', 'col')), parts along dimension 0, may hold values from 0 to 23, as said below
- tile_count: int32 [192], P(('slab', 'col')), parts along dimension 0, may hold values from 8 to 12
- candidates: int32 [192, 12], P(('slab', 'col')), parts along dimension 0, may hold values from 0 to 95, as said below
- degree: int32 [192, 128], P(('slab', 'col')), parts along dimension 0, may hold values from 8 to 64
Outputs:
- snn_weights: bfloat16 [192, 12, 128, 128], P(('slab', 'col')), parts along dimension 0
The draws below stay inside these ranges and needn't reach their ends.
There are 2 independent parts, one for each index of `slab`. The reference program is written for one: setup_inputs(seed, part) draws one part's arguments, and reference() takes and returns one part's arrays. A program takes and returns all parts, laid end to end along the dimension named above; each array names one. Nothing has to cross between parts.
Inputs may be any that keep to these rules, and one draw needn't show every extreme that they name: `tile_cols`: the 12 column blocks of a block row are distinct. The 12 candidates of a block row are distinct; the candidates of the 6 block rows of one device, taken together, name exactly one block row of each aligned range of 6 block rows.
All inputs are finite; a program needn't handle non-finite values.
Results may differ from the reference program's by a relative error of at most 0.001.
Values may be sent and summed in bfloat16 or wider, within the bound.
No kernel may reach another device: no remote copies, remote signals or barrier semaphores. Data moves between devices by JAX's collectives and lax.ppermute only.
A program may use at most 128 MiB of HBM per device.

```python
import jax
import jax.numpy as jnp
from jax import lax

TILE = 128
R = 12
KB = 24
Q = 12
BR = 6
NB = 96


def draw_tile_cols(key, part):
    key = jax.random.fold_in(key, 1)
    common_key, pick_key, order_key = jax.random.split(key, 3)
    hub_total = 5 * R // 6
    column_ids = jnp.arange(KB, dtype=jnp.int32)
    common_scores = jax.random.randint(common_key, (KB,), 0, 2 ** 20) * KB + column_ids
    common_rank = jnp.argsort(jnp.argsort(common_scores))
    is_common = (common_rank < hub_total).astype(jnp.int32)
    row_scores = jax.random.randint(pick_key, (NB, KB), 0, 2 ** 20)
    scores = ((1 - is_common)[None, :] * 2 ** 20 + row_scores) * KB + column_ids[None, :]
    chosen = jnp.argsort(scores, axis=1)[:, :R].astype(jnp.int32)
    slot_scores = jax.random.randint(order_key, (NB, R), 0, 2 ** 20) * R + jnp.arange(R, dtype=jnp.int32)[None, :]
    slot_order = jnp.argsort(slot_scores, axis=1)
    return jnp.take_along_axis(chosen, slot_order, axis=1).astype(jnp.int32)


def draw_candidates(key, part):
    key = jax.random.fold_in(key, 2)
    first_key, second_key = jax.random.split(key)
    groups = NB // BR
    group_ids = jnp.arange(groups, dtype=jnp.int32)
    pool = group_ids[None, :] * BR + jax.random.randint(first_key, (groups, groups), 0, BR)
    scores = jax.random.randint(second_key, (groups, groups), 0, 2 ** 20) * groups + group_ids[None, :]
    order = jnp.argsort(scores, axis=1)
    picked = jnp.take_along_axis(pool, order, axis=1)
    positions = (jnp.arange(BR, dtype=jnp.int32)[:, None] * Q + jnp.arange(Q, dtype=jnp.int32)[None, :]) % groups
    chosen = picked[:, positions]
    return chosen.reshape(NB, Q).astype(jnp.int32)


def with_ends(result, key, low, high):
    index_at = [jax.random.randint(jax.random.fold_in(key, axis), (), 0, length) for axis, length in enumerate(result.shape)]
    longest = result.shape.index(max(result.shape))
    beside = index_at[:longest] + [(index_at[longest] + 1) % result.shape[longest]] + index_at[longest + 1:]
    return result.at[tuple(index_at)].set(low).at[tuple(beside)].set(high)


def levels(rng, dims, cuts, least, high):
    level = 1.0
    for axis_at, blocks in cuts:
        heights = jax.random.uniform(jax.random.fold_in(jax.random.fold_in(rng, 6), axis_at), (blocks,), jnp.float32, least / len(cuts), high / len(cuts))
        level = level * jnp.repeat(jnp.exp(heights), dims[axis_at] // blocks).reshape((-1,) + (1,) * (len(dims) - 1 - axis_at))
    return level


def noise(key, dims, scale, reach, cuts=(), kind=jnp.bfloat16):
    result = scale * jax.random.normal(key, dims, jnp.float32)
    if cuts:
        result = result * levels(key, dims, cuts, -0.22, 0.18)
    return jnp.clip(result, -reach, reach).astype(kind)


def setup_inputs(seed: int = 0, part: int = 0) -> dict:
    seeds = jax.random.split(jax.random.key(seed), 6)
    part_splits = jax.random.split(jax.random.fold_in(seeds[5], part), 6)
    return {
        "tiles": noise(part_splits[0], (NB, R, TILE, TILE), 1.0, 6.0, ((0, 16),)),
        "tile_cols": draw_tile_cols(jax.random.fold_in(jax.random.fold_in(seeds[5], part), 71), part),
        "tile_count": with_ends(jax.random.randint(part_splits[2], (NB,), (2 * R) // 3, R + 1), jax.random.fold_in(part_splits[2], 1), (2 * R) // 3, R).astype(jnp.int32),
        "candidates": draw_candidates(jax.random.fold_in(jax.random.fold_in(seeds[5], part), 71), part),
        "degree": with_ends(jax.random.randint(part_splits[4], (NB, TILE), 8, 65), jax.random.fold_in(part_splits[4], 1), 8, 64).astype(jnp.int32),
    }


def reference(tiles, tile_cols, tile_count, candidates, degree):
    slot_ids = jnp.arange(R, dtype=jnp.int32)

    def row_output(inputs):
        row_tiles, row_cols, row_total, row_cands, row_degree = inputs
        other_tiles = tiles[row_cands]
        other_cols = tile_cols[row_cands]
        other_total = tile_count[row_cands]
        other_degree = degree[row_cands]
        live_row = slot_ids < row_total
        live_other = slot_ids[None, :] < other_total[:, None]
        matches = (row_cols[None, :, None] == other_cols[:, None, :]) & live_row[None, :, None] & live_other[:, None, :]
        match_mask = matches.astype(jnp.float32)
        matched = jnp.einsum('qrs,qsyk->qryk', match_mask, other_tiles.astype(jnp.float32))
        shared = jnp.einsum('rxk,qryk->qxy', row_tiles.astype(jnp.float32), matched)
        product = row_degree.astype(jnp.float32)[None, :, None] * other_degree.astype(jnp.float32)[:, None, :]
        return (shared / jnp.sqrt(product)).astype(jnp.bfloat16)
    return lax.map(row_output, (tiles, tile_cols, tile_count, candidates, degree))
```

```python
import functools

import jax
import jax.numpy as jnp
from jax import lax
from jax.experimental import pallas as pl
from jax.experimental.pallas import tpu as pltpu
from jax.sharding import PartitionSpec as P

VMEM_LIMIT = 48 * 1024 * 1024


def pick_rows_kernel(rows_ref, tiles_ref, out_ref, sems):
    for k in range(out_ref.shape[0]):
        pltpu.make_async_copy(tiles_ref.at[rows_ref[k]], out_ref.at[k], sems.at[k]).start()
    for k in range(out_ref.shape[0]):
        pltpu.make_async_copy(tiles_ref.at[0], out_ref.at[k], sems.at[k]).wait()


def pick_rows(rows, tiles):
    total = rows.shape[0]
    return pl.pallas_call(
        pick_rows_kernel,
        out_shape=jax.ShapeDtypeStruct((total,) + tiles.shape[1:], tiles.dtype),
        in_specs=[pl.BlockSpec(memory_space=pltpu.SMEM), pl.BlockSpec(memory_space=pl.ANY)],
        out_specs=pl.BlockSpec(memory_space=pl.ANY),
        scratch_shapes=[pltpu.SemaphoreType.DMA((total,))],
        name="pick_rows",
    )(rows, tiles)


def blocks_kernel(owner_ref, slot_ref, tiles_ref, fetched_ref, scale_row_ref, scale_other_ref, out_ref):
    local_rows, slots, side, _ = tiles_ref.shape
    cands = out_ref.shape[1]

    def one_row(i, carry):
        left = jnp.concatenate([tiles_ref[i, r] for r in range(slots)], axis=1)
        scale_x = jnp.broadcast_to(scale_row_ref[i], (side, side)).T

        def one_block(q, inner):
            owner = owner_ref[i * cands + q]
            picked = []
            for r in range(slots):
                s = slot_ref[(i * cands + q) * slots + r]
                tile = fetched_ref[owner, jnp.maximum(s, 0)]
                picked.append(jnp.where(s >= 0, tile, jnp.zeros_like(tile)))
            right = jnp.concatenate(picked, axis=1)
            shared = lax.dot_general(left, right, (((1,), (1,)), ((), ())), preferred_element_type=jnp.float32)
            out_ref[i, q] = (shared * (scale_x * scale_other_ref[owner])).astype(out_ref.dtype)
            return inner

        return lax.fori_loop(0, cands, one_block, carry, unroll=2)

    lax.fori_loop(0, local_rows, one_row, 0)


def blocks(owners, slot_of, tiles, fetched, scale_row, scale_other):
    local_rows, slots, side, _ = tiles.shape
    cands = owners.shape[1]
    smem = pl.BlockSpec(memory_space=pltpu.SMEM)
    vmem = pl.BlockSpec(memory_space=pltpu.VMEM)
    return pl.pallas_call(
        blocks_kernel,
        out_shape=jax.ShapeDtypeStruct((local_rows, cands, side, side), jnp.bfloat16),
        in_specs=[smem, smem, vmem, vmem, vmem, vmem],
        out_specs=vmem,
        compiler_params=pltpu.CompilerParams(vmem_limit_bytes=VMEM_LIMIT),
        name="blocks",
    )(owners.reshape(-1), slot_of.reshape(-1), tiles, fetched, scale_row[:, None, :], scale_other[:, None, :])


def local(tiles, tile_cols, tile_count, candidates, degree):
    local_rows, slots, side, _ = tiles.shape
    peers = lax.axis_size("col")
    me = lax.axis_index("col")
    owners = candidates // local_rows
    peer_ids = jnp.arange(peers, dtype=jnp.int32)
    row_ids = jnp.arange(local_rows, dtype=jnp.int32)

    matches = owners[:, :, None] == peer_ids
    wanted = jnp.max(jnp.where(matches, (candidates % local_rows)[:, :, None], 0), axis=(0, 1))

    note = jnp.concatenate([wanted, tile_count, tile_cols.reshape(-1), degree.reshape(-1)])
    note = jnp.pad(note, (0, -note.shape[0] % 128))
    notes = lax.all_to_all(
        jnp.broadcast_to(note, (peers, note.shape[0])), "col", split_axis=0, concat_axis=0, tiled=True
    )
    asked = lax.dynamic_index_in_dim(notes, me, axis=1, keepdims=False)
    at = peers
    counts_all = notes[:, at : at + local_rows]
    at += local_rows
    cols_all = notes[:, at : at + local_rows * slots].reshape(peers, local_rows, slots)
    at += local_rows * slots
    degree_all = notes[:, at : at + local_rows * side].reshape(peers, local_rows, side)

    send = pick_rows(asked, tiles)
    fetched = lax.all_to_all(send, "col", split_axis=0, concat_axis=0, tiled=True)

    mine = wanted[:, None] == row_ids
    count_got = jnp.sum(jnp.where(mine, counts_all, 0), axis=1)
    cols_got = jnp.sum(jnp.where(mine[:, :, None], cols_all, 0), axis=1)
    degree_got = jnp.sum(jnp.where(mine[:, :, None], degree_all, 0), axis=1)
    slot_ids = jnp.arange(slots, dtype=jnp.int32)
    cols_got = jnp.where(slot_ids < count_got[:, None], cols_got, -1)
    cols_other = jnp.sum(jnp.where(matches[..., None], cols_got, 0), axis=2)
    cols_mine = jnp.where(slot_ids < tile_count[:, None], tile_cols, -2)
    meets = cols_mine[:, None, :, None] == cols_other[:, :, None, :]
    slot_of = jnp.sum(jnp.where(meets, slot_ids + 1, 0), axis=3) - 1

    scale_row = lax.rsqrt(degree.astype(jnp.float32))
    scale_other = lax.rsqrt(degree_got.astype(jnp.float32))
    return blocks(owners, slot_of, tiles, fetched, scale_row, scale_other)


def solution(mesh):
    in_specs = (
        P(("slab", "col"), None, None, None),
        P(("slab", "col"), None),
        P(("slab", "col")),
        P(("slab", "col"), None),
        P(("slab", "col"), None),
    )
    out_specs = P(("slab", "col"), None, None, None)
    return jax.shard_map(local, mesh=mesh, in_specs=in_specs, out_specs=out_specs, check_vma=False)
```

```python
import functools

import jax
import jax.numpy as jnp
from jax import lax
from jax.experimental import pallas as pl
from jax.experimental.pallas import tpu as pltpu
from jax.sharding import PartitionSpec as P

VMEM_LIMIT = 48 * 1024 * 1024


def pick_rows_kernel(rows_ref, tiles_ref, out_ref, sems):
    for k in range(out_ref.shape[0]):
        pltpu.make_async_copy(tiles_ref.at[rows_ref[k]], out_ref.at[k], sems.at[k]).start()
    for k in range(out_ref.shape[0]):
        pltpu.make_async_copy(tiles_ref.at[0], out_ref.at[k], sems.at[k]).wait()


def pick_rows(rows, tiles):
    total = rows.shape[0]
    return pl.pallas_call(
        pick_rows_kernel,
        out_shape=jax.ShapeDtypeStruct((total,) + tiles.shape[1:], tiles.dtype),
        in_specs=[pl.BlockSpec(memory_space=pltpu.SMEM), pl.BlockSpec(memory_space=pltpu.VMEM)],
        out_specs=pl.BlockSpec(memory_space=pl.ANY),
        scratch_shapes=[pltpu.SemaphoreType.DMA((total,))],
        compiler_params=pltpu.CompilerParams(vmem_limit_bytes=VMEM_LIMIT),
        name="pick_rows",
    )(rows, tiles)


def blocks_kernel(owner_ref, slot_ref, tiles_ref, fetched_ref, scale_row_ref, scale_other_ref, out_ref):
    local_rows, slots, side, _ = tiles_ref.shape
    cands = out_ref.shape[1]

    def one_row(i, carry):
        left = jnp.concatenate([tiles_ref[i, r] for r in range(slots)], axis=1)
        scale_x = jnp.broadcast_to(scale_row_ref[i], (side, side)).T

        def one_block(q, inner):
            owner = owner_ref[i * cands + q]
            picked = []
            for r in range(slots):
                s = slot_ref[(i * cands + q) * slots + r]
                tile = fetched_ref[owner, jnp.maximum(s, 0)]
                picked.append(jnp.where(s >= 0, tile, jnp.zeros_like(tile)))
            right = jnp.concatenate(picked, axis=1)
            shared = lax.dot_general(left, right, (((1,), (1,)), ((), ())), preferred_element_type=jnp.float32)
            out_ref[i, q] = (shared * (scale_x * scale_other_ref[owner])).astype(out_ref.dtype)
            return inner

        return lax.fori_loop(0, cands, one_block, carry, unroll=2)

    lax.fori_loop(0, local_rows, one_row, 0)


def blocks(owners, slot_of, tiles, fetched, scale_row, scale_other):
    local_rows, slots, side, _ = tiles.shape
    cands = owners.shape[1]
    smem = pl.BlockSpec(memory_space=pltpu.SMEM)
    vmem = pl.BlockSpec(memory_space=pltpu.VMEM)
    return pl.pallas_call(
        blocks_kernel,
        out_shape=jax.ShapeDtypeStruct((local_rows, cands, side, side), jnp.bfloat16),
        in_specs=[smem, smem, vmem, vmem, vmem, vmem],
        out_specs=vmem,
        compiler_params=pltpu.CompilerParams(vmem_limit_bytes=VMEM_LIMIT),
        name="blocks",
    )(owners.reshape(-1), slot_of.reshape(-1), tiles, fetched, scale_row[:, None, :], scale_other[:, None, :])


def local(tiles, tile_cols, tile_count, candidates, degree):
    local_rows, slots, side, _ = tiles.shape
    peers = lax.axis_size("col")
    me = lax.axis_index("col")
    owners = candidates // local_rows
    peer_ids = jnp.arange(peers, dtype=jnp.int32)
    row_ids = jnp.arange(local_rows, dtype=jnp.int32)

    matches = owners[:, :, None] == peer_ids
    wanted = jnp.max(jnp.where(matches, (candidates % local_rows)[:, :, None], 0), axis=(0, 1))

    note = jnp.concatenate([wanted, tile_count, tile_cols.reshape(-1), degree.reshape(-1)])
    note = jnp.pad(note, (0, -note.shape[0] % 128))
    notes = lax.all_to_all(
        jnp.broadcast_to(note, (peers, note.shape[0])), "col", split_axis=0, concat_axis=0, tiled=True
    )
    asked = lax.dynamic_index_in_dim(notes, me, axis=1, keepdims=False)
    at = peers
    counts_all = notes[:, at : at + local_rows]
    at += local_rows
    cols_all = notes[:, at : at + local_rows * slots].reshape(peers, local_rows, slots)
    at += local_rows * slots
    degree_all = notes[:, at : at + local_rows * side].reshape(peers, local_rows, side)

    send = pick_rows(asked, tiles)
    fetched = lax.all_to_all(send, "col", split_axis=0, concat_axis=0, tiled=True)

    mine = wanted[:, None] == row_ids
    count_got = jnp.sum(jnp.where(mine, counts_all, 0), axis=1)
    cols_got = jnp.sum(jnp.where(mine[:, :, None], cols_all, 0), axis=1)
    degree_got = jnp.sum(jnp.where(mine[:, :, None], degree_all, 0), axis=1)
    slot_ids = jnp.arange(slots, dtype=jnp.int32)
    cols_got = jnp.where(slot_ids < count_got[:, None], cols_got, -1)
    cols_other = jnp.sum(jnp.where(matches[..., None], cols_got, 0), axis=2)
    cols_mine = jnp.where(slot_ids < tile_count[:, None], tile_cols, -2)
    meets = cols_mine[:, None, :, None] == cols_other[:, :, None, :]
    slot_of = jnp.sum(jnp.where(meets, slot_ids + 1, 0), axis=3) - 1

    scale_row = lax.rsqrt(degree.astype(jnp.float32))
    scale_other = lax.rsqrt(degree_got.astype(jnp.float32))
    return blocks(owners, slot_of, tiles, fetched, scale_row, scale_other)


def solution(mesh):
    in_specs = (
        P(("slab", "col"), None, None, None),
        P(("slab", "col"), None),
        P(("slab", "col")),
        P(("slab", "col"), None),
        P(("slab", "col"), None),
    )
    out_specs = P(("slab", "col"), None, None, None)
    return jax.shard_map(local, mesh=mesh, in_specs=in_specs, out_specs=out_specs, check_vma=False)
```

```python
import functools

import jax
import jax.numpy as jnp
from jax import lax
from jax.experimental import pallas as pl
from jax.experimental.pallas import tpu as pltpu
from jax.sharding import PartitionSpec as P

VMEM_LIMIT = 48 * 1024 * 1024
SMEM = pl.BlockSpec(memory_space=pltpu.SMEM)
VMEM = pl.BlockSpec(memory_space=pltpu.VMEM)
HBM = pl.BlockSpec(memory_space=pl.ANY)
PARAMS = pltpu.CompilerParams(vmem_limit_bytes=VMEM_LIMIT)


def pick_rows_kernel(sizes, rows_ref, tiles_ref, *refs):
    outs, sems = refs[:-1], refs[-1]
    places = [(ref, k) for ref, size in zip(outs, sizes) for k in range(size)]
    for at, (ref, k) in enumerate(places):
        pltpu.make_async_copy(tiles_ref.at[rows_ref[at]], ref.at[k], sems.at[at]).start()
    for at, (ref, k) in enumerate(places):
        pltpu.make_async_copy(tiles_ref.at[0], ref.at[k], sems.at[at]).wait()


def pick_rows(rows, tiles, sizes):
    return pl.pallas_call(
        functools.partial(pick_rows_kernel, sizes),
        out_shape=[jax.ShapeDtypeStruct((size,) + tiles.shape[1:], tiles.dtype) for size in sizes],
        in_specs=[SMEM, VMEM],
        out_specs=[HBM] * len(sizes),
        scratch_shapes=[pltpu.SemaphoreType.DMA((sum(sizes),))],
        compiler_params=PARAMS,
        name="pick_rows",
    )(rows, tiles)


def fetch_rows(total, source_ref, row_ref, sources, target_ref, sems):
    for k in range(total):
        for at, ref in enumerate(sources):

            last = at == len(sources) - 1

            @pl.when(source_ref[k] >= at if last else source_ref[k] == at)
            def _():
                pltpu.make_async_copy(ref.at[row_ref[k]], target_ref.at[k], sems.at[k]).start()

    for k in range(total):
        pltpu.make_async_copy(sources[0].at[0], target_ref.at[k], sems.at[k]).wait()


def collect_kernel(total, source_ref, row_ref, *refs):
    *sources, out_ref, sems = refs
    fetch_rows(total, source_ref, row_ref, sources, out_ref, sems)


def collect(places, *sources):
    total = len(places)
    source_ids = jnp.stack([jnp.asarray(s, jnp.int32) for s, _ in places])
    row_ids = jnp.stack([jnp.asarray(row, jnp.int32) for _, row in places])
    return pl.pallas_call(
        functools.partial(collect_kernel, total),
        out_shape=jax.ShapeDtypeStruct((total,) + sources[0].shape[1:], sources[0].dtype),
        in_specs=[SMEM, SMEM] + [HBM] * len(sources),
        out_specs=VMEM,
        scratch_shapes=[pltpu.SemaphoreType.DMA((total,))],
        compiler_params=PARAMS,
        name="collect",
    )(source_ids, row_ids, *sources)


def blocks_kernel(total, prior, place_ref, slot_ref, source_ref, row_ref, tiles_ref, scale_row_ref, scale_got_ref, *refs):
    *sources, out_ref, fetched_ref, sems = refs
    if prior:
        prior_ref, *sources = sources
    local_rows, slots, side, _ = tiles_ref.shape
    cands = out_ref.shape[1]
    fetch_rows(total, source_ref, row_ref, sources, fetched_ref, sems)

    def one_row(i, carry):
        left = jnp.concatenate([tiles_ref[i, r] for r in range(slots)], axis=1)
        scale_x = jnp.broadcast_to(scale_row_ref[i], (side, side)).T

        def one_block(q, inner):
            place = place_ref[i * cands + q]

            @pl.when(place >= 0)
            def _():
                picked = []
                for r in range(slots):
                    s = slot_ref[(i * cands + q) * slots + r]
                    tile = fetched_ref[place, jnp.maximum(s, 0)]
                    picked.append(jnp.where(s >= 0, tile, jnp.zeros_like(tile)))
                right = jnp.concatenate(picked, axis=1)
                shared = lax.dot_general(left, right, (((1,), (1,)), ((), ())), preferred_element_type=jnp.float32)
                out_ref[i, q] = (shared * (scale_x * scale_got_ref[place])).astype(out_ref.dtype)

            if prior:

                @pl.when(place < 0)
                def _():
                    out_ref[i, q] = prior_ref[i, q]

            return inner

        return lax.fori_loop(0, cands, one_block, carry, unroll=2)

    lax.fori_loop(0, local_rows, one_row, 0)


def blocks(place, slot_of, places, tiles, scale_row, scale_got, sources, prior=None):
    local_rows, slots, side, _ = tiles.shape
    total = len(places)
    source_ids = jnp.stack([jnp.asarray(s, jnp.int32) for s, _ in places])
    row_ids = jnp.stack([jnp.asarray(row, jnp.int32) for _, row in places])
    extra = [] if prior is None else [prior]
    return pl.pallas_call(
        functools.partial(blocks_kernel, total, prior is not None),
        out_shape=jax.ShapeDtypeStruct((local_rows, place.shape[1], side, side), jnp.bfloat16),
        in_specs=[SMEM] * 4 + [VMEM] * (3 + len(extra)) + [HBM] * len(sources),
        out_specs=VMEM,
        scratch_shapes=[
            pltpu.VMEM((total,) + tiles.shape[1:], tiles.dtype),
            pltpu.SemaphoreType.DMA((total,)),
        ],
        compiler_params=PARAMS,
        name="blocks",
    )(
        place.reshape(-1), slot_of.reshape(-1), source_ids, row_ids, tiles, scale_row[:, None, :], scale_got[:, None, :],
        *extra, *sources,
    )


def exchange_direct(wanted_by, me, tiles):
    asked = lax.dynamic_index_in_dim(wanted_by, me, axis=1, keepdims=False)
    (send,) = pick_rows(asked, tiles, (asked.shape[0],))
    return lax.all_to_all(send, "col", split_axis=0, concat_axis=0, tiled=True)


def moves(target):
    return [(4 * z + p, 4 * target[z] + p) for z in range(4) for p in range(4) if target[z] is not None]


BESIDE = moves([1, 0, 3, 2])
MIDDLE = moves([None, 2, 1, None])
ACROSS = moves([2, None, None, 1])
OUTWARD = moves([None, 0, 3, None])
Y_MATE = [(i, i ^ 2) for i in range(16)]
CORE_MATE = [(i, i ^ 1) for i in range(16)]


def relay(wanted_by, me, tiles, make_blocks):
    plane, mate = me // 4, me % 4
    inner = (plane == 1) | (plane == 2)

    def want(to_plane, m, from_plane):
        return wanted_by[4 * to_plane + (mate ^ m), 4 * from_plane + mate]

    outer = jnp.where(inner, plane ^ 2, plane)
    row_ids = jnp.arange(tiles.shape[0], dtype=jnp.int32)
    key = row_ids + 4
    for at, m in ((3, 1), (2, 0), (1, 3), (0, 2)):
        key = jnp.where(row_ids == want(outer ^ 3, m, outer), at, key)
    rank = jnp.sum((key[None, :] < key[:, None]).astype(jnp.int32), axis=1)
    order = jnp.sum(jnp.where(rank[None, :] == row_ids[:, None], row_ids[None, :], 0), axis=1)

    def rank_of(row):
        return jnp.sum(jnp.where(row_ids == row, rank, 0))

    middle = lax.ppermute(tiles, "col", MIDDLE)
    rows = [want(plane ^ 1, m, plane) for m in range(4)] + [want(plane, m, plane) for m in (2, 3, 0, 1)]
    beside_send, y1_send, own = pick_rows(jnp.stack(rows), tiles, (4, 2, 2))
    beside = lax.ppermute(beside_send, "col", BESIDE)
    y1 = lax.ppermute(y1_send, "col", Y_MATE)
    far_send = pick_rows(order, tiles, (2, 2, 2))
    far = [lax.ppermute(part, "col", ACROSS) for part in far_send]

    out_send = collect([(0, want(plane ^ 1, m, plane ^ 3)) for m in range(4)], middle)
    out_near = lax.ppermute(out_send, "col", OUTWARD)
    y2 = lax.ppermute(collect([(0, 2), (0, 3)], beside), "col", Y_MATE)

    def far_place(row):
        at = rank_of(row)
        return at // 2, at % 2

    g1_send = collect([far_place(want(plane ^ 1, m, plane ^ 2)) for m in (2, 3)], *far[:1])
    g1 = lax.ppermute(g1_send, "col", OUTWARD)
    g2_send = collect([far_place(want(plane ^ 1, m, plane ^ 2)) for m in (0, 1)], *far[:2])
    g2 = lax.ppermute(g2_send, "col", OUTWARD)

    core_a = lax.ppermute(collect([(0, 1), (1, 1), (2, 1), (3, 1)], own, y1, beside, y2), "col", CORE_MATE)
    done = make_blocks(
        (0, 1), [(0, 0), (4, 0), (1, 0), (4, 1), (2, 0), (4, 2), (3, 0), (4, 3)], (own, y1, beside, y2, core_a), None
    )

    def third(m):
        return jnp.where(inner, 0, 1), jnp.where(inner, want(plane, m, plane ^ 3), m)

    y3 = lax.ppermute(collect([third(2), third(3)], middle, out_near), "col", Y_MATE)
    core_b = lax.ppermute(collect([third(1), (2, 1)], middle, out_near, y3), "col", CORE_MATE)
    done = make_blocks((2,), [third(0), (3, 0), (2, 0), (3, 1)], (middle, out_near, y3, core_b), done)

    def fourth(m):
        at = rank_of(want(plane, m, plane ^ 2))
        return jnp.where(inner, at // 2, 3), jnp.where(inner, at % 2, m % 2)

    y4 = lax.ppermute(collect([fourth(2), fourth(3)], *far, g1), "col", Y_MATE)
    core_c = lax.ppermute(collect([fourth(1), (4, 1)], *far, g2, y4), "col", CORE_MATE)
    return make_blocks((3,), [fourth(0), (5, 0), (4, 0), (5, 1)], (*far, g2, y4, core_c), done)


def local(tiles, tile_cols, tile_count, candidates, degree):
    local_rows, slots, side, _ = tiles.shape
    peers = lax.axis_size("col")
    me = lax.axis_index("col")
    owners = candidates // local_rows
    peer_ids = jnp.arange(peers, dtype=jnp.int32)
    row_ids = jnp.arange(local_rows, dtype=jnp.int32)

    matches = owners[:, :, None] == peer_ids
    wanted = jnp.max(jnp.where(matches, (candidates % local_rows)[:, :, None], 0), axis=(0, 1))

    note = jnp.concatenate([wanted, tile_count, tile_cols.reshape(-1), degree.reshape(-1)])
    note = jnp.pad(note, (0, -note.shape[0] % 128))
    notes = lax.all_to_all(
        jnp.broadcast_to(note, (peers, note.shape[0])), "col", split_axis=0, concat_axis=0, tiled=True
    )
    wanted_by = notes[:, :peers]
    at = peers
    counts_all = notes[:, at : at + local_rows]
    at += local_rows
    cols_all = notes[:, at : at + local_rows * slots].reshape(peers, local_rows, slots)
    at += local_rows * slots
    degree_all = notes[:, at : at + local_rows * side].reshape(peers, local_rows, side)

    mine = wanted[:, None] == row_ids
    count_got = jnp.sum(jnp.where(mine, counts_all, 0), axis=1)
    cols_got = jnp.sum(jnp.where(mine[:, :, None], cols_all, 0), axis=1)
    degree_got = jnp.sum(jnp.where(mine[:, :, None], degree_all, 0), axis=1)
    slot_ids = jnp.arange(slots, dtype=jnp.int32)
    cols_got = jnp.where(slot_ids < count_got[:, None], cols_got, -1)
    cols_other = jnp.sum(jnp.where(matches[..., None], cols_got, 0), axis=2)
    cols_mine = jnp.where(slot_ids < tile_count[:, None], tile_cols, -2)
    meets = cols_mine[:, None, :, None] == cols_other[:, :, None, :]
    slot_of = jnp.sum(jnp.where(meets, slot_ids + 1, 0), axis=3) - 1

    scale_row = lax.rsqrt(degree.astype(jnp.float32))
    scale_other = lax.rsqrt(degree_got.astype(jnp.float32))

    if peers != 16:
        fetched = exchange_direct(wanted_by, me, tiles)
        places = [(0, k) for k in range(peers)]
        return blocks(owners, slot_of, places, tiles, scale_row, scale_other, [fetched])

    plane, mate = me // 4, me % 4
    inner = (plane == 1) | (plane == 2)
    group_planes = [plane, plane ^ 1, jnp.where(inner, plane ^ 3, plane ^ 2), jnp.where(inner, plane ^ 2, plane ^ 3)]

    def make_blocks(groups, places, sources, prior):
        place = jnp.full_like(owners, -1)
        for at, group in enumerate(groups):
            place = jnp.where(owners // 4 == group_planes[group], 4 * at + (mate ^ (owners % 4)), place)
        owner_of = jnp.concatenate([4 * group_planes[g] + (mate ^ jnp.arange(4, dtype=jnp.int32)) for g in groups])
        scale_got = jnp.sum(jnp.where((owner_of[:, None] == peer_ids)[:, :, None], scale_other, 0.0), axis=1)
        return blocks(place, slot_of, places, tiles, scale_row, scale_got, sources, prior)

    return relay(wanted_by, me, tiles, make_blocks)


def solution(mesh):
    in_specs = (
        P(("slab", "col"), None, None, None),
        P(("slab", "col"), None),
        P(("slab", "col")),
        P(("slab", "col"), None),
        P(("slab", "col"), None),
    )
    out_specs = P(("slab", "col"), None, None, None)
    return jax.shard_map(local, mesh=mesh, in_specs=in_specs, out_specs=out_specs, check_vma=False)
```

```python
import functools

import jax
import jax.numpy as jnp
from jax import lax
from jax.experimental import pallas as pl
from jax.experimental.pallas import tpu as pltpu
from jax.sharding import PartitionSpec as P

VMEM_LIMIT = 48 * 1024 * 1024
SMEM = pl.BlockSpec(memory_space=pltpu.SMEM)
VMEM = pl.BlockSpec(memory_space=pltpu.VMEM)
HBM = pl.BlockSpec(memory_space=pl.ANY)
PARAMS = pltpu.CompilerParams(vmem_limit_bytes=VMEM_LIMIT)


def pick_rows_kernel(sizes, rows_ref, tiles_ref, *refs):
    outs, sems = refs[:-1], refs[-1]
    places = [(ref, k) for ref, size in zip(outs, sizes) for k in range(size)]
    for at, (ref, k) in enumerate(places):
        pltpu.make_async_copy(tiles_ref.at[rows_ref[at]], ref.at[k], sems.at[at]).start()
    for at, (ref, k) in enumerate(places):
        pltpu.make_async_copy(tiles_ref.at[0], ref.at[k], sems.at[at]).wait()


def pick_rows(rows, tiles, sizes):
    return pl.pallas_call(
        functools.partial(pick_rows_kernel, sizes),
        out_shape=[jax.ShapeDtypeStruct((size,) + tiles.shape[1:], tiles.dtype) for size in sizes],
        in_specs=[SMEM, VMEM],
        out_specs=[HBM] * len(sizes),
        scratch_shapes=[pltpu.SemaphoreType.DMA((sum(sizes),))],
        compiler_params=PARAMS,
        name="pick_rows",
    )(rows, tiles)


def fetch_rows(total, source_ref, row_ref, sources, target_ref, sems):
    for k in range(total):
        for at, ref in enumerate(sources):

            last = at == len(sources) - 1

            @pl.when(source_ref[k] >= at if last else source_ref[k] == at)
            def _():
                pltpu.make_async_copy(ref.at[row_ref[k]], target_ref.at[k], sems.at[k]).start()

    for k in range(total):
        pltpu.make_async_copy(sources[0].at[0], target_ref.at[k], sems.at[k]).wait()


def collect_kernel(total, source_ref, row_ref, *refs):
    sources, outs, sems = refs[: -1 - total], refs[-1 - total : -1], refs[-1]
    for at, ref in enumerate(sources):

        @pl.when(source_ref[0] == at)
        def _():
            for k in range(total):
                pltpu.make_async_copy(ref.at[row_ref[k]], outs[k].at[0], sems.at[k]).start()

    for k in range(total):
        pltpu.make_async_copy(sources[0].at[0], outs[k].at[0], sems.at[k]).wait()


def collect_each(source, rows, *sources):
    total = rows.shape[0]
    return pl.pallas_call(
        functools.partial(collect_kernel, total),
        out_shape=[jax.ShapeDtypeStruct((1,) + sources[0].shape[1:], sources[0].dtype)] * total,
        in_specs=[SMEM, SMEM] + [HBM] * len(sources),
        out_specs=[VMEM] * total,
        scratch_shapes=[pltpu.SemaphoreType.DMA((total,))],
        compiler_params=PARAMS,
        name="collect",
    )(source[None], rows, *sources)


def blocks_kernel(total, owner_ref, slot_ref, source_ref, row_ref, tiles_ref, scale_row_ref, scale_got_ref, *refs):
    *sources, out_ref, fetched_ref, sems = refs
    local_rows, slots, side, _ = tiles_ref.shape
    cands = out_ref.shape[1]
    together = 2 if cands % 2 == 0 else 1
    fetch_rows(total, source_ref, row_ref, sources, fetched_ref, sems)

    def one_row(i, carry):
        left = jnp.concatenate([tiles_ref[i, r] for r in range(slots)], axis=1)
        scale_x = jnp.broadcast_to(scale_row_ref[i], (side, side)).T

        def some_blocks(step, inner):
            right = []
            for k in range(together):
                block = i * cands + step * together + k
                owner = owner_ref[block]
                picked = []
                for r in range(slots):
                    s = slot_ref[block * slots + r]
                    tile = fetched_ref[owner, jnp.maximum(s, 0)]
                    picked.append(jnp.where(s >= 0, tile, jnp.zeros_like(tile)))
                right.append(jnp.concatenate(picked, axis=1))
            right = jnp.concatenate(right, axis=0)
            shared = lax.dot_general(left, right, (((1,), (1,)), ((), ())), preferred_element_type=jnp.float32)
            for k in range(together):
                q = step * together + k
                scale = scale_x * scale_got_ref[owner_ref[i * cands + q]]
                out_ref[i, q] = (shared[:, k * side : (k + 1) * side] * scale).astype(out_ref.dtype)
            return inner

        return lax.fori_loop(0, cands // together, some_blocks, carry)

    lax.fori_loop(0, local_rows, one_row, 0)


def blocks(owners, slot_of, source_ids, row_ids, tiles, scale_row, scale_got, sources):
    local_rows, slots, side, _ = tiles.shape
    total = source_ids.shape[0]
    return pl.pallas_call(
        functools.partial(blocks_kernel, total),
        out_shape=jax.ShapeDtypeStruct((local_rows, owners.shape[1], side, side), jnp.bfloat16),
        in_specs=[SMEM] * 4 + [VMEM] * 3 + [HBM] * len(sources),
        out_specs=VMEM,
        scratch_shapes=[
            pltpu.VMEM((total,) + tiles.shape[1:], tiles.dtype),
            pltpu.SemaphoreType.DMA((total,)),
        ],
        compiler_params=PARAMS,
        name="blocks",
    )(
        owners.reshape(-1), slot_of.reshape(-1), source_ids, row_ids, tiles, scale_row[:, None, :], scale_got[:, None, :],
        *sources,
    )


def exchange_direct(wanted_by, me, tiles):
    asked = lax.dynamic_index_in_dim(wanted_by, me, axis=1, keepdims=False)
    (send,) = pick_rows(asked, tiles, (asked.shape[0],))
    return lax.all_to_all(send, "col", split_axis=0, concat_axis=0, tiled=True)


def moves(targets, flip=0):
    return [(4 * z + p, 4 * t + (p ^ flip)) for z, t in enumerate(targets) if t is not None for p in range(4)]


HALVES = [list(range(8)), list(range(8, 16))]


def relay(wanted_by, me, tiles, middle):
    plane, mate = me // 4, me % 4
    inner = (plane == 1) | (plane == 2)
    flips = jnp.arange(4, dtype=jnp.int32)
    peer_ids = jnp.arange(16, dtype=jnp.int32)

    def lookup(readers, owner):
        of_owner = jnp.sum(jnp.where(peer_ids == owner, wanted_by, 0), axis=1)
        return jnp.sum(jnp.where(readers[:, None] == peer_ids, of_owner, 0), axis=1)

    half = me // 8 * 8 + jnp.arange(8, dtype=jnp.int32)
    beyond = 4 * (plane ^ 3) + (mate ^ flips)
    half_send, first_send = pick_rows(lookup(jnp.concatenate([half, beyond[:1]]), me), tiles, (8, 1))
    near = lax.all_to_all(half_send, "col", split_axis=0, concat_axis=0, axis_index_groups=HALVES, tiled=True)
    beyond_got = [lax.ppermute(first_send, "col", moves([3, None, None, 0]))]

    readers = jnp.concatenate(
        [jnp.where(inner, 4 * plane, 4 * (plane ^ 3)) + (mate ^ flips[1:]),
         jnp.where(inner, 4 * (plane ^ 1), 4 * (plane ^ 2)) + (mate ^ flips)]
    )
    rows = lookup(readers, jnp.where(inner, 4 * (plane ^ 3) + mate, me))
    sends = collect_each(jnp.where(inner, 1, 0), rows, tiles, middle)
    beyond_got += [lax.ppermute(sends[m - 1], "col", moves([3, 1, 2, 0], m)) for m in (1, 2, 3)]
    across_got = [lax.ppermute(sends[m + 3], "col", moves([2, 0, 3, 1], m)) for m in range(4)]

    mine_in_middle = lookup(me[None], 4 * (plane ^ 3) + mate)[0]
    owner_plane, flip = peer_ids // 4, mate ^ (peer_ids % 4)
    is_near, is_beyond = owner_plane // 2 == plane // 2, owner_plane == plane ^ 3
    is_middle = is_beyond & inner & (flip == 0)
    source_ids = jnp.where(is_near, 0, jnp.where(is_middle, 1, jnp.where(is_beyond, 2, 6) + flip))
    row_ids = jnp.where(is_near, peer_ids % 8, jnp.where(is_middle, mine_in_middle, 0))
    return source_ids, row_ids, [near, middle, *beyond_got, *across_got]


def local(tiles, tile_cols, tile_count, candidates, degree):
    local_rows, slots, side, _ = tiles.shape
    peers = lax.axis_size("col")
    me = lax.axis_index("col")
    owners = candidates // local_rows
    peer_ids = jnp.arange(peers, dtype=jnp.int32)
    row_ids = jnp.arange(local_rows, dtype=jnp.int32)

    matches = owners[:, :, None] == peer_ids
    wanted = jnp.max(jnp.where(matches, (candidates % local_rows)[:, :, None], 0), axis=(0, 1))

    note = jnp.concatenate([wanted, tile_count, tile_cols.reshape(-1), degree.reshape(-1)])
    note = jnp.pad(note, (0, -note.shape[0] % 128))
    note = jnp.broadcast_to(note, (peers, note.shape[0]))
    relayed = peers == 16
    if relayed:
        tiles_behind, note = lax.optimization_barrier((tiles, note))
    notes = lax.all_to_all(note, "col", split_axis=0, concat_axis=0, tiled=True)
    if relayed:
        middle = lax.ppermute(tiles_behind, "col", moves([None, 2, 1, None]))
    wanted_by = notes[:, :peers]
    at = peers
    counts_all = notes[:, at : at + local_rows]
    at += local_rows
    cols_all = notes[:, at : at + local_rows * slots].reshape(peers, local_rows, slots)
    at += local_rows * slots
    degree_all = notes[:, at : at + local_rows * side].reshape(peers, local_rows, side)

    mine = wanted[:, None] == row_ids
    count_got = jnp.sum(jnp.where(mine, counts_all, 0), axis=1)
    cols_got = jnp.sum(jnp.where(mine[:, :, None], cols_all, 0), axis=1)
    degree_got = jnp.sum(jnp.where(mine[:, :, None], degree_all, 0), axis=1)
    slot_ids = jnp.arange(slots, dtype=jnp.int32)
    cols_got = jnp.where(slot_ids < count_got[:, None], cols_got, -1)
    cols_other = jnp.sum(jnp.where(matches[..., None], cols_got, 0), axis=2)
    cols_mine = jnp.where(slot_ids < tile_count[:, None], tile_cols, -2)
    meets = cols_mine[:, None, :, None] == cols_other[:, :, None, :]
    slot_of = jnp.sum(jnp.where(meets, slot_ids + 1, 0), axis=3) - 1

    scale_row = lax.rsqrt(degree.astype(jnp.float32))
    scale_other = lax.rsqrt(degree_got.astype(jnp.float32))

    if relayed:
        source_ids, row_ids, sources = relay(wanted_by, me, tiles, middle)
    else:
        sources = [exchange_direct(wanted_by, me, tiles)]
        source_ids, row_ids = jnp.zeros_like(peer_ids), peer_ids
    return blocks(owners, slot_of, source_ids, row_ids, tiles, scale_row, scale_other, sources)


def solution(mesh):
    in_specs = (
        P(("slab", "col"), None, None, None),
        P(("slab", "col"), None),
        P(("slab", "col")),
        P(("slab", "col"), None),
        P(("slab", "col"), None),
    )
    out_specs = P(("slab", "col"), None, None, None)
    return jax.shard_map(local, mesh=mesh, in_specs=in_specs, out_specs=out_specs, check_vma=False)
```

```python
import functools

import jax
import jax.numpy as jnp
from jax import lax
from jax.experimental import pallas as pl
from jax.experimental.pallas import tpu as pltpu
from jax.sharding import PartitionSpec as P

VMEM_LIMIT = 48 * 1024 * 1024
SMEM = pl.BlockSpec(memory_space=pltpu.SMEM)
VMEM = pl.BlockSpec(memory_space=pltpu.VMEM)
HBM = pl.BlockSpec(memory_space=pl.ANY)
PARAMS = pltpu.CompilerParams(vmem_limit_bytes=VMEM_LIMIT)


def pick_rows_kernel(sizes, rows_ref, tiles_ref, *refs):
    outs, sems = refs[:-1], refs[-1]
    places = [(ref, k) for ref, size in zip(outs, sizes) for k in range(size)]
    for at, (ref, k) in enumerate(places):
        pltpu.make_async_copy(tiles_ref.at[rows_ref[at]], ref.at[k], sems.at[at]).start()
    for at, (ref, k) in enumerate(places):
        pltpu.make_async_copy(tiles_ref.at[0], ref.at[k], sems.at[at]).wait()


def pick_rows(rows, tiles, sizes):
    return pl.pallas_call(
        functools.partial(pick_rows_kernel, sizes),
        out_shape=[jax.ShapeDtypeStruct((size,) + tiles.shape[1:], tiles.dtype) for size in sizes],
        in_specs=[SMEM, VMEM],
        out_specs=[HBM] * len(sizes),
        scratch_shapes=[pltpu.SemaphoreType.DMA((sum(sizes),))],
        compiler_params=PARAMS,
        name="pick_rows",
    )(rows, tiles)


def start_rows(total, source_ref, row_ref, sources, target_ref, sems):
    for k in range(total):
        for at, ref in enumerate(sources):
            last = at == len(sources) - 1

            @pl.when(source_ref[k] >= at if last else source_ref[k] == at)
            def _():
                pltpu.make_async_copy(ref.at[row_ref[k]], target_ref.at[k], sems.at[k]).start()


def wait_rows(total, sources, target_ref, sems):
    for k in range(total):
        pltpu.make_async_copy(sources[0].at[0], target_ref.at[k], sems.at[k]).wait()


def stack_kernel(total, source_ref, row_ref, *refs):
    *sources, out_ref, sems = refs
    start_rows(total, source_ref, row_ref, sources, out_ref, sems)
    wait_rows(total, sources, out_ref, sems)


def stack_rows(source_ids, row_ids, *sources):
    total = source_ids.shape[0]
    return pl.pallas_call(
        functools.partial(stack_kernel, total),
        out_shape=jax.ShapeDtypeStruct((total,) + sources[0].shape[1:], sources[0].dtype),
        in_specs=[SMEM, SMEM] + [HBM] * len(sources),
        out_specs=VMEM,
        scratch_shapes=[pltpu.SemaphoreType.DMA((total,))],
        compiler_params=PARAMS,
        name="stack_rows",
    )(source_ids, row_ids, *sources)


def collect_kernel(total, source_ref, row_ref, *refs):
    sources, outs, sems = refs[: -1 - total], refs[-1 - total : -1], refs[-1]
    for at, ref in enumerate(sources):

        @pl.when(source_ref[0] == at)
        def _():
            for k in range(total):
                pltpu.make_async_copy(ref.at[row_ref[k]], outs[k].at[0], sems.at[k]).start()

    for k in range(total):
        pltpu.make_async_copy(sources[0].at[0], outs[k].at[0], sems.at[k]).wait()


def collect_each(source, rows, *sources):
    total = rows.shape[0]
    return pl.pallas_call(
        functools.partial(collect_kernel, total),
        out_shape=[jax.ShapeDtypeStruct((1,) + sources[0].shape[1:], sources[0].dtype)] * total,
        in_specs=[SMEM, SMEM] + [HBM] * len(sources),
        out_specs=[VMEM] * total,
        scratch_shapes=[pltpu.SemaphoreType.DMA((total,))],
        compiler_params=PARAMS,
        name="collect",
    )(source[None], rows, *sources)


def blocks_kernel(total, prior, place_ref, slot_ref, source_ref, row_ref, tiles_ref, scale_row_ref, scale_got_ref, *refs):
    *sources, out_ref, fetched_ref, scale_ref, stage_ref, list_ref, sems, out_sems = refs
    if prior:
        sources = sources[1:]
    local_rows, slots, side, _ = tiles_ref.shape
    cands = out_ref.shape[1]
    start_rows(total, source_ref, row_ref, sources, fetched_ref, sems)

    def note_block(block, count):
        place = place_ref[block]

        @pl.when(place >= 0)
        def _():
            list_ref[count] = block

        return count + (place >= 0).astype(jnp.int32)

    count = lax.fori_loop(0, local_rows * cands, note_block, jnp.int32(0))
    for i in range(local_rows):
        scale_ref[i] = jnp.broadcast_to(scale_row_ref[i], (side, side)).T
    wait_rows(total, sources, fetched_ref, sems)

    def two_blocks(step, carry):
        for k in (0, 1):
            at = 2 * step + k
            block = list_ref[jnp.minimum(at, count - 1)]
            i, place = block // cands, place_ref[block]
            left, right = [], []
            for r in range(slots):
                s = slot_ref[block * slots + r]
                tile = fetched_ref[place, jnp.maximum(s, 0)]
                right.append(jnp.where(s >= 0, tile, jnp.zeros_like(tile)))
                left.append(tiles_ref[i, r])
            shared = lax.dot_general(
                jnp.concatenate(left, axis=1), jnp.concatenate(right, axis=1), (((1,), (1,)), ((), ())),
                preferred_element_type=jnp.float32,
            )
            stage_ref[at] = (shared * (scale_ref[i] * scale_got_ref[place])).astype(stage_ref.dtype)
        for k in (0, 1):
            at = 2 * step + k

            @pl.when(at < count)
            def _():
                block = list_ref[at]
                to = out_ref.at[block // cands, lax.rem(block, cands)]
                pltpu.make_async_copy(stage_ref.at[at], to, out_sems.at[at]).start()

        return carry

    lax.fori_loop(0, (count + 1) // 2, two_blocks, 0)

    def wait_block(at, carry):
        pltpu.make_async_copy(stage_ref.at[at], out_ref.at[0, 0], out_sems.at[at]).wait()
        return carry

    lax.fori_loop(0, count, wait_block, 0)


def blocks(place, slot_of, source_ids, row_ids, tiles, scale_row, scale_got, sources, prior=None):
    local_rows, slots, side, _ = tiles.shape
    total, cands = source_ids.shape[0], place.shape[1]
    every = local_rows * cands
    extra = [] if prior is None else [prior]
    return pl.pallas_call(
        functools.partial(blocks_kernel, total, prior is not None),
        out_shape=jax.ShapeDtypeStruct((local_rows, cands, side, side), jnp.bfloat16),
        in_specs=[SMEM] * 4 + [VMEM] * 3 + [HBM] * (len(extra) + len(sources)),
        out_specs=HBM,
        input_output_aliases={7: 0} if extra else {},
        scratch_shapes=[
            pltpu.VMEM((total,) + tiles.shape[1:], tiles.dtype),
            pltpu.VMEM((local_rows, side, side), jnp.float32),
            pltpu.VMEM((every + every % 2, side, side), jnp.bfloat16),
            pltpu.SMEM((every,), jnp.int32),
            pltpu.SemaphoreType.DMA((total,)),
            pltpu.SemaphoreType.DMA((every,)),
        ],
        compiler_params=PARAMS,
        cost_estimate=pl.CostEstimate(
            flops=2 * total * every // 16 * slots * side**3, bytes_accessed=2 * (total + local_rows) * slots * side**2,
            transcendentals=0,
        ),
        name="blocks",
    )(
        place.reshape(-1), slot_of.reshape(-1), source_ids, row_ids, tiles, scale_row[:, None, :], scale_got[:, None, :],
        *extra, *sources,
    )


def exchange_direct(wanted_by, me, tiles):
    asked = lax.dynamic_index_in_dim(wanted_by, me, axis=1, keepdims=False)
    (send,) = pick_rows(asked, tiles, (asked.shape[0],))
    return lax.all_to_all(send, "col", split_axis=0, concat_axis=0, tiled=True)


def moves(targets, flip=0):
    return [(4 * z + p, 4 * t + (p ^ flip)) for z, t in enumerate(targets) if t is not None for p in range(4)]


PLANES = [[4 * z + p for p in range(4)] for z in range(4)]


def relay(wanted_by, me, tiles, middle):
    plane, mate = me // 4, me % 4
    inner = (plane == 1) | (plane == 2)
    flips = jnp.arange(4, dtype=jnp.int32)
    peer_ids = jnp.arange(16, dtype=jnp.int32)

    def lookup(readers, owner):
        of_owner = jnp.sum(jnp.where(peer_ids == owner, wanted_by, 0), axis=1)
        return jnp.sum(jnp.where(readers[:, None] == peer_ids, of_owner, 0), axis=1)

    beyond = 4 * (plane ^ 3) + (mate ^ flips)
    readers = jnp.concatenate([4 * (plane ^ 1) + flips, beyond[:1], 4 * plane + flips])
    mine = lookup(readers, me)
    beside_send, first_send = pick_rows(mine[:5], tiles, (4, 1))
    beside = lax.ppermute(beside_send, "col", moves([1, 0, 3, 2]))
    beyond_got = [lax.ppermute(first_send, "col", moves([3, None, None, 0]))]
    pairs = jnp.arange(8, dtype=jnp.int32)
    rows = jnp.where(pairs % 2 == 0, jnp.repeat(mine[5:], 2), pairs // 2)
    plane_send = stack_rows(pairs % 2, rows, tiles, beside)
    near = lax.all_to_all(plane_send, "col", split_axis=0, concat_axis=0, axis_index_groups=PLANES, tiled=True)

    readers = jnp.concatenate(
        [jnp.where(inner, 4 * plane, 4 * (plane ^ 3)) + (mate ^ flips[1:]),
         jnp.where(inner, 4 * (plane ^ 1), 4 * (plane ^ 2)) + (mate ^ flips)]
    )
    rows = lookup(readers, jnp.where(inner, 4 * (plane ^ 3) + mate, me))
    sends = collect_each(jnp.where(inner, 1, 0), rows, tiles, middle)
    beyond_got += [lax.ppermute(sends[m - 1], "col", moves([3, 1, 2, 0], m)) for m in (1, 2, 3)]
    across_got = [lax.ppermute(sends[m + 3], "col", moves([2, 0, 3, 1], m)) for m in range(4)]

    first_owners = jnp.concatenate([jnp.where(pairs % 2 == 0, 4 * plane, 4 * (plane ^ 1)) + pairs // 2, beyond])
    mine_in_middle = lookup(me[None], beyond[0])
    sources = jnp.concatenate([jnp.zeros((8,), jnp.int32), jnp.where(inner & (flips == 0), 1, 2 + flips)])
    rows = jnp.concatenate([pairs, jnp.where(inner & (flips == 0), mine_in_middle, 0)])
    return [
        (first_owners, sources, rows, [near, middle, *beyond_got]),
        (4 * (plane ^ 2) + (mate ^ flips), flips, jnp.zeros_like(flips), across_got),
    ]


def local(tiles, tile_cols, tile_count, candidates, degree):
    local_rows, slots, side, _ = tiles.shape
    peers = lax.axis_size("col")
    me = lax.axis_index("col")
    owners = candidates // local_rows
    peer_ids = jnp.arange(peers, dtype=jnp.int32)
    row_ids = jnp.arange(local_rows, dtype=jnp.int32)

    matches = owners[:, :, None] == peer_ids
    wanted = jnp.max(jnp.where(matches, (candidates % local_rows)[:, :, None], 0), axis=(0, 1))

    note = jnp.concatenate([wanted, tile_count, tile_cols.reshape(-1), degree.reshape(-1)])
    note = jnp.pad(note, (0, -note.shape[0] % 128))
    note = jnp.broadcast_to(note, (peers, note.shape[0]))
    relayed = peers == 16
    if relayed:
        tiles_behind, note = lax.optimization_barrier((tiles, note))
    notes = lax.all_to_all(note, "col", split_axis=0, concat_axis=0, tiled=True)
    if relayed:
        middle = lax.ppermute(tiles_behind, "col", moves([None, 2, 1, None]))
    wanted_by = notes[:, :peers]
    at = peers
    counts_all = notes[:, at : at + local_rows]
    at += local_rows
    cols_all = notes[:, at : at + local_rows * slots].reshape(peers, local_rows, slots)
    at += local_rows * slots
    degree_all = notes[:, at : at + local_rows * side].reshape(peers, local_rows, side)

    mine = wanted[:, None] == row_ids
    count_got = jnp.sum(jnp.where(mine, counts_all, 0), axis=1)
    cols_got = jnp.sum(jnp.where(mine[:, :, None], cols_all, 0), axis=1)
    degree_got = jnp.sum(jnp.where(mine[:, :, None], degree_all, 0), axis=1)
    slot_ids = jnp.arange(slots, dtype=jnp.int32)
    cols_got = jnp.where(slot_ids < count_got[:, None], cols_got, -1)
    cols_other = jnp.sum(jnp.where(matches[..., None], cols_got, 0), axis=2)
    cols_mine = jnp.where(slot_ids < tile_count[:, None], tile_cols, -2)
    meets = cols_mine[:, None, :, None] == cols_other[:, :, None, :]
    slot_of = jnp.sum(jnp.where(meets, slot_ids + 1, 0), axis=3) - 1

    scale_row = lax.rsqrt(degree.astype(jnp.float32))
    scale_other = lax.rsqrt(degree_got.astype(jnp.float32))

    if relayed:
        parts = relay(wanted_by, me, tiles, middle)
    else:
        parts = [(peer_ids, jnp.zeros_like(peer_ids), peer_ids, [exchange_direct(wanted_by, me, tiles)])]
    done = None
    for owner_ids, source_ids, row_ids, sources in parts:
        at = jnp.arange(owner_ids.shape[0], dtype=jnp.int32)
        place = jnp.sum(jnp.where(owners[:, :, None] == owner_ids, at + 1, 0), axis=2) - 1
        scale_got = jnp.sum(jnp.where((owner_ids[:, None] == peer_ids)[:, :, None], scale_other, 0.0), axis=1)
        done = blocks(place, slot_of, source_ids, row_ids, tiles, scale_row, scale_got, sources, done)
    return done


def solution(mesh):
    in_specs = (
        P(("slab", "col"), None, None, None),
        P(("slab", "col"), None),
        P(("slab", "col")),
        P(("slab", "col"), None),
        P(("slab", "col"), None),
    )
    out_specs = P(("slab", "col"), None, None, None)
    return jax.shard_map(local, mesh=mesh, in_specs=in_specs, out_specs=out_specs, check_vma=False)
```

```python
import functools

import jax
import jax.numpy as jnp
from jax import lax
from jax.experimental import pallas as pl
from jax.experimental.pallas import tpu as pltpu
from jax.sharding import PartitionSpec as P

VMEM_LIMIT = 48 * 1024 * 1024
SMEM = pl.BlockSpec(memory_space=pltpu.SMEM)
VMEM = pl.BlockSpec(memory_space=pltpu.VMEM)
HBM = pl.BlockSpec(memory_space=pl.ANY)
PARAMS = pltpu.CompilerParams(vmem_limit_bytes=VMEM_LIMIT)


def pick_rows_kernel(sizes, rows_ref, tiles_ref, *refs):
    outs, sems = refs[:-1], refs[-1]
    places = [(ref, k) for ref, size in zip(outs, sizes) for k in range(size)]
    for at, (ref, k) in enumerate(places):
        pltpu.make_async_copy(tiles_ref.at[rows_ref[at]], ref.at[k], sems.at[at]).start()
    for at, (ref, k) in enumerate(places):
        pltpu.make_async_copy(tiles_ref.at[0], ref.at[k], sems.at[at]).wait()


def pick_rows(rows, tiles, sizes):
    return pl.pallas_call(
        functools.partial(pick_rows_kernel, sizes),
        out_shape=[jax.ShapeDtypeStruct((size,) + tiles.shape[1:], tiles.dtype) for size in sizes],
        in_specs=[SMEM, VMEM],
        out_specs=[HBM] * len(sizes),
        scratch_shapes=[pltpu.SemaphoreType.DMA((sum(sizes),))],
        compiler_params=PARAMS,
        name="pick_rows",
    )(rows, tiles)


def start_rows(total, source_ref, row_ref, sources, target_ref, sems):
    for k in range(total):
        for at, ref in enumerate(sources):
            last = at == len(sources) - 1

            @pl.when(source_ref[k] >= at if last else source_ref[k] == at)
            def _():
                pltpu.make_async_copy(ref.at[row_ref[k]], target_ref.at[k], sems.at[k]).start()


def wait_rows(total, sources, target_ref, sems):
    for k in range(total):
        pltpu.make_async_copy(sources[0].at[0], target_ref.at[k], sems.at[k]).wait()


def stack_kernel(total, source_ref, row_ref, *refs):
    *sources, out_ref, sems = refs
    start_rows(total, source_ref, row_ref, sources, out_ref, sems)
    wait_rows(total, sources, out_ref, sems)


def stack_rows(source_ids, row_ids, *sources):
    total = source_ids.shape[0]
    return pl.pallas_call(
        functools.partial(stack_kernel, total),
        out_shape=jax.ShapeDtypeStruct((total,) + sources[0].shape[1:], sources[0].dtype),
        in_specs=[SMEM, SMEM] + [HBM] * len(sources),
        out_specs=VMEM,
        scratch_shapes=[pltpu.SemaphoreType.DMA((total,))],
        compiler_params=PARAMS,
        name="stack_rows",
    )(source_ids, row_ids, *sources)


def collect_kernel(total, source_ref, row_ref, *refs):
    sources, outs, sems = refs[: -1 - total], refs[-1 - total : -1], refs[-1]
    for at, ref in enumerate(sources):

        @pl.when(source_ref[0] == at)
        def _():
            for k in range(total):
                pltpu.make_async_copy(ref.at[row_ref[k]], outs[k].at[0], sems.at[k]).start()

    for k in range(total):
        pltpu.make_async_copy(sources[0].at[0], outs[k].at[0], sems.at[k]).wait()


def collect_each(source, rows, *sources):
    total = rows.shape[0]
    return pl.pallas_call(
        functools.partial(collect_kernel, total),
        out_shape=[jax.ShapeDtypeStruct((1,) + sources[0].shape[1:], sources[0].dtype)] * total,
        in_specs=[SMEM, SMEM] + [HBM] * len(sources),
        out_specs=[VMEM] * total,
        scratch_shapes=[pltpu.SemaphoreType.DMA((total,))],
        compiler_params=PARAMS,
        name="collect",
    )(source[None], rows, *sources)


def blocks_kernel(total, prior, place_ref, slot_ref, source_ref, row_ref, tiles_ref, scale_row_ref, scale_got_ref, *refs):
    *sources, out_ref, fetched_ref, scale_ref, stage_ref, list_ref, sems, out_sems = refs
    if prior:
        sources = sources[1:]
    local_rows, slots, side, _ = tiles_ref.shape
    cands = out_ref.shape[1]
    start_rows(total, source_ref, row_ref, sources, fetched_ref, sems)

    def note_block(block, count):
        place = place_ref[block]

        @pl.when(place >= 0)
        def _():
            list_ref[count] = block

        return count + (place >= 0).astype(jnp.int32)

    count = lax.fori_loop(0, local_rows * cands, note_block, jnp.int32(0))
    for i in range(local_rows):
        scale_ref[i] = jnp.broadcast_to(scale_row_ref[i], (side, side)).T
    wait_rows(total, sources, fetched_ref, sems)

    def two_blocks(step, carry):
        for k in (0, 1):
            at = 2 * step + k
            block = list_ref[jnp.minimum(at, count - 1)]
            i, place = block // cands, place_ref[block]
            left, right = [], []
            for r in range(slots):
                s = slot_ref[block * slots + r]
                tile = fetched_ref[place, jnp.maximum(s, 0)]
                right.append(jnp.where(s >= 0, tile, jnp.zeros_like(tile)))
                left.append(tiles_ref[i, r])
            shared = lax.dot_general(
                jnp.concatenate(left, axis=1), jnp.concatenate(right, axis=1), (((1,), (1,)), ((), ())),
                preferred_element_type=jnp.float32,
            )
            stage_ref[at] = (shared * (scale_ref[i] * scale_got_ref[place])).astype(stage_ref.dtype)
        for k in (0, 1):
            at = 2 * step + k

            @pl.when(at < count)
            def _():
                block = list_ref[at]
                to = out_ref.at[block // cands, lax.rem(block, cands)]
                pltpu.make_async_copy(stage_ref.at[at], to, out_sems.at[at]).start()

        return carry

    lax.fori_loop(0, (count + 1) // 2, two_blocks, 0)

    def wait_block(at, carry):
        pltpu.make_async_copy(stage_ref.at[at], out_ref.at[0, 0], out_sems.at[at]).wait()
        return carry

    lax.fori_loop(0, count, wait_block, 0)


def blocks(place, slot_of, source_ids, row_ids, tiles, scale_row, scale_got, sources, prior=None):
    local_rows, slots, side, _ = tiles.shape
    total, cands = source_ids.shape[0], place.shape[1]
    every = local_rows * cands
    extra = [] if prior is None else [prior]
    return pl.pallas_call(
        functools.partial(blocks_kernel, total, prior is not None),
        out_shape=jax.ShapeDtypeStruct((local_rows, cands, side, side), jnp.bfloat16),
        in_specs=[SMEM] * 4 + [VMEM] * 3 + [HBM] * (len(extra) + len(sources)),
        out_specs=HBM,
        input_output_aliases={7: 0} if extra else {},
        scratch_shapes=[
            pltpu.VMEM((total,) + tiles.shape[1:], tiles.dtype),
            pltpu.VMEM((local_rows, side, side), jnp.float32),
            pltpu.VMEM((every + every % 2, side, side), jnp.bfloat16),
            pltpu.SMEM((every,), jnp.int32),
            pltpu.SemaphoreType.DMA((total,)),
            pltpu.SemaphoreType.DMA((every,)),
        ],
        compiler_params=PARAMS,
        cost_estimate=pl.CostEstimate(
            flops=2 * total * every // 16 * slots * side**3, bytes_accessed=2 * (total + local_rows) * slots * side**2,
            transcendentals=0,
        ),
        name="blocks",
    )(
        place.reshape(-1), slot_of.reshape(-1), source_ids, row_ids, tiles, scale_row[:, None, :], scale_got[:, None, :],
        *extra, *sources,
    )


def exchange_direct(wanted_by, me, tiles):
    asked = lax.dynamic_index_in_dim(wanted_by, me, axis=1, keepdims=False)
    (send,) = pick_rows(asked, tiles, (asked.shape[0],))
    return lax.all_to_all(send, "col", split_axis=0, concat_axis=0, tiled=True)


def moves(targets, flip=0):
    return [(4 * z + p, 4 * t + (p ^ flip)) for z, t in enumerate(targets) if t is not None for p in range(4)]


PLANES = [[4 * z + p for p in range(4)] for z in range(4)]


def relay(wanted_by, me, tiles, middle):
    plane, mate = me // 4, me % 4
    inner = (plane == 1) | (plane == 2)
    flips = jnp.arange(4, dtype=jnp.int32)
    peer_ids = jnp.arange(16, dtype=jnp.int32)

    def lookup(readers, owner):
        of_owner = jnp.sum(jnp.where(peer_ids == owner, wanted_by, 0), axis=1)
        return jnp.sum(jnp.where(readers[:, None] == peer_ids, of_owner, 0), axis=1)

    beyond = 4 * (plane ^ 3) + (mate ^ flips)
    mine = lookup(jnp.concatenate([4 * (plane ^ 1) + flips, 4 * plane + flips, beyond[:1]]), me)
    (beside_send,) = pick_rows(mine[:4], tiles, (4,))
    beside = lax.ppermute(beside_send, "col", moves([1, 0, 3, 2]))
    own_send, first_send = pick_rows(mine[4:], tiles, (4, 1))
    own = lax.all_to_all(own_send, "col", split_axis=0, concat_axis=0, axis_index_groups=PLANES, tiled=True)
    near = lax.all_to_all(beside, "col", split_axis=0, concat_axis=0, axis_index_groups=PLANES, tiled=True)
    beyond_got = [lax.ppermute(first_send, "col", moves([3, None, None, 0]))]

    readers = jnp.concatenate(
        [jnp.where(inner, 4 * plane, 4 * (plane ^ 3)) + (mate ^ flips[1:]),
         jnp.where(inner, 4 * (plane ^ 1), 4 * (plane ^ 2)) + (mate ^ flips)]
    )
    rows = lookup(readers, jnp.where(inner, 4 * (plane ^ 3) + mate, me))
    sends = collect_each(jnp.where(inner, 1, 0), rows, tiles, middle)
    beyond_got += [lax.ppermute(sends[m - 1], "col", moves([3, 1, 2, 0], m)) for m in (1, 2, 3)]
    across_got = [lax.ppermute(sends[m + 3], "col", moves([2, 0, 3, 1], m)) for m in range(4)]

    near_owners = jnp.concatenate([4 * plane + flips, 4 * (plane ^ 1) + flips])
    across = 4 * (plane ^ 2) + (mate ^ flips)
    from_middle = inner & (flips == 0)
    two, none = flips[:2], 0 * flips
    return [
        (near_owners, jnp.concatenate([none, none + 1]), jnp.concatenate([flips, flips]), [own, near]),
        (
            jnp.concatenate([beyond, across[:2]]),
            jnp.concatenate([jnp.where(from_middle, 0, 1 + flips), 5 + two]),
            jnp.concatenate([jnp.where(from_middle, lookup(me[None], beyond[0]), 0), none[:2]]),
            [middle, *beyond_got, *across_got[:2]],
        ),
        (across[2:], two, none[:2], across_got[2:]),
    ]


def local(tiles, tile_cols, tile_count, candidates, degree):
    local_rows, slots, side, _ = tiles.shape
    peers = lax.axis_size("col")
    me = lax.axis_index("col")
    owners = candidates // local_rows
    peer_ids = jnp.arange(peers, dtype=jnp.int32)
    row_ids = jnp.arange(local_rows, dtype=jnp.int32)

    matches = owners[:, :, None] == peer_ids
    wanted = jnp.max(jnp.where(matches, (candidates % local_rows)[:, :, None], 0), axis=(0, 1))

    note = jnp.concatenate([wanted, tile_count, tile_cols.reshape(-1), degree.reshape(-1)])
    note = jnp.pad(note, (0, -note.shape[0] % 128))
    note = jnp.broadcast_to(note, (peers, note.shape[0]))
    relayed = peers == 16
    if relayed:
        tiles_behind, note = lax.optimization_barrier((tiles, note))
    notes = lax.all_to_all(note, "col", split_axis=0, concat_axis=0, tiled=True)
    if relayed:
        middle = lax.ppermute(tiles_behind, "col", moves([None, 2, 1, None]))
    wanted_by = notes[:, :peers]
    at = peers
    counts_all = notes[:, at : at + local_rows]
    at += local_rows
    cols_all = notes[:, at : at + local_rows * slots].reshape(peers, local_rows, slots)
    at += local_rows * slots
    degree_all = notes[:, at : at + local_rows * side].reshape(peers, local_rows, side)

    mine = wanted[:, None] == row_ids
    count_got = jnp.sum(jnp.where(mine, counts_all, 0), axis=1)
    cols_got = jnp.sum(jnp.where(mine[:, :, None], cols_all, 0), axis=1)
    degree_got = jnp.sum(jnp.where(mine[:, :, None], degree_all, 0), axis=1)
    slot_ids = jnp.arange(slots, dtype=jnp.int32)
    cols_got = jnp.where(slot_ids < count_got[:, None], cols_got, -1)
    cols_other = jnp.sum(jnp.where(matches[..., None], cols_got, 0), axis=2)
    cols_mine = jnp.where(slot_ids < tile_count[:, None], tile_cols, -2)
    meets = cols_mine[:, None, :, None] == cols_other[:, :, None, :]
    slot_of = jnp.sum(jnp.where(meets, slot_ids + 1, 0), axis=3) - 1

    scale_row = lax.rsqrt(degree.astype(jnp.float32))
    scale_other = lax.rsqrt(degree_got.astype(jnp.float32))

    if relayed:
        parts = relay(wanted_by, me, tiles, middle)
    else:
        parts = [(peer_ids, jnp.zeros_like(peer_ids), peer_ids, [exchange_direct(wanted_by, me, tiles)])]
    done = None
    for owner_ids, source_ids, row_ids, sources in parts:
        at = jnp.arange(owner_ids.shape[0], dtype=jnp.int32)
        place = jnp.sum(jnp.where(owners[:, :, None] == owner_ids, at + 1, 0), axis=2) - 1
        scale_got = jnp.sum(jnp.where((owner_ids[:, None] == peer_ids)[:, :, None], scale_other, 0.0), axis=1)
        done = blocks(place, slot_of, source_ids, row_ids, tiles, scale_row, scale_got, sources, done)
    return done


def solution(mesh):
    in_specs = (
        P(("slab", "col"), None, None, None),
        P(("slab", "col"), None),
        P(("slab", "col")),
        P(("slab", "col"), None),
        P(("slab", "col"), None),
    )
    out_specs = P(("slab", "col"), None, None, None)
    return jax.shard_map(local, mesh=mesh, in_specs=in_specs, out_specs=out_specs, check_vma=False)
```

```python
import functools

import jax
import jax.numpy as jnp
from jax import lax
from jax.experimental import pallas as pl
from jax.experimental.pallas import tpu as pltpu
from jax.sharding import PartitionSpec as P

VMEM_LIMIT = 48 * 1024 * 1024
SMEM = pl.BlockSpec(memory_space=pltpu.SMEM)
VMEM = pl.BlockSpec(memory_space=pltpu.VMEM)
HBM = pl.BlockSpec(memory_space=pl.ANY)
PARAMS = pltpu.CompilerParams(vmem_limit_bytes=VMEM_LIMIT)
WHOLE_VMEM = pltpu.CompilerParams(vmem_limit_bytes=62 * 1024 * 1024)


def start_rows(total, source_ref, row_ref, sources, target_ref, sems):
    for k in range(total):
        for at, ref in enumerate(sources):
            last = at == len(sources) - 1

            @pl.when(source_ref[k] >= at if last else source_ref[k] == at)
            def _():
                pltpu.make_async_copy(ref.at[row_ref[k]], target_ref.at[k], sems.at[k]).start()


def wait_rows(total, sources, target_ref, sems):
    for k in range(total):
        pltpu.make_async_copy(sources[0].at[0], target_ref.at[k], sems.at[k]).wait()


def move_rows_kernel(sizes, source_ref, row_ref, *refs):
    *sources, stage_ref, sems, out_sems = refs
    sources, outs = sources[: -len(sizes)], sources[-len(sizes) :]
    places = [ref.at[k] for ref, size in zip(outs, sizes) for k in range(size)]
    start_rows(len(places), source_ref, row_ref, sources, stage_ref, sems)
    for k, place in enumerate(places):
        pltpu.make_async_copy(sources[0].at[0], stage_ref.at[k], sems.at[k]).wait()
        pltpu.make_async_copy(stage_ref.at[k], place, out_sems.at[k]).start()
    for k, place in enumerate(places):
        pltpu.make_async_copy(stage_ref.at[k], place, out_sems.at[k]).wait()


def move_rows(source_ids, row_ids, sizes, *sources):
    row, dtype = sources[0].shape[1:], sources[0].dtype
    return pl.pallas_call(
        functools.partial(move_rows_kernel, sizes),
        out_shape=[jax.ShapeDtypeStruct((size,) + row, dtype) for size in sizes],
        in_specs=[SMEM, SMEM] + [HBM] * len(sources),
        out_specs=[HBM] * len(sizes),
        scratch_shapes=[
            pltpu.VMEM((sum(sizes),) + row, dtype),
            pltpu.SemaphoreType.DMA((sum(sizes),)),
            pltpu.SemaphoreType.DMA((sum(sizes),)),
        ],
        compiler_params=WHOLE_VMEM,
        name="move_rows",
    )(source_ids, row_ids, *sources)


def pick_rows(rows, tiles, sizes):
    return move_rows(jnp.zeros_like(rows), rows, sizes, tiles)


def blocks_kernel(total, prior, place_ref, slot_ref, source_ref, row_ref, tiles_ref, scale_row_ref, scale_got_ref, *refs):
    *sources, out_ref, fetched_ref, scale_ref, stage_ref, list_ref, sems, out_sems = refs
    if prior:
        sources = sources[1:]
    local_rows, slots, side, _ = tiles_ref.shape
    cands = out_ref.shape[1]
    start_rows(total, source_ref, row_ref, sources, fetched_ref, sems)

    def note_block(block, count):
        place = place_ref[block]

        @pl.when(place >= 0)
        def _():
            list_ref[count] = block

        return count + (place >= 0).astype(jnp.int32)

    count = lax.fori_loop(0, local_rows * cands, note_block, jnp.int32(0))
    for i in range(local_rows):
        scale_ref[i] = jnp.broadcast_to(scale_row_ref[i], (side, side)).T
    wait_rows(total, sources, fetched_ref, sems)

    def two_blocks(step, carry):
        for k in (0, 1):
            at = 2 * step + k
            block = list_ref[jnp.minimum(at, count - 1)]
            i, place = block // cands, place_ref[block]
            left, right = [], []
            for r in range(slots):
                s = slot_ref[block * slots + r]
                tile = fetched_ref[place, jnp.maximum(s, 0)]
                right.append(jnp.where(s >= 0, tile, jnp.zeros_like(tile)))
                left.append(tiles_ref[i, r])
            shared = lax.dot_general(
                jnp.concatenate(left, axis=1), jnp.concatenate(right, axis=1), (((1,), (1,)), ((), ())),
                preferred_element_type=jnp.float32,
            )
            stage_ref[at] = (shared * (scale_ref[i] * scale_got_ref[place])).astype(stage_ref.dtype)
        for k in (0, 1):
            at = 2 * step + k

            @pl.when(at < count)
            def _():
                block = list_ref[at]
                to = out_ref.at[block // cands, lax.rem(block, cands)]
                pltpu.make_async_copy(stage_ref.at[at], to, out_sems.at[at]).start()

        return carry

    lax.fori_loop(0, (count + 1) // 2, two_blocks, 0)

    def wait_block(at, carry):
        pltpu.make_async_copy(stage_ref.at[at], out_ref.at[0, 0], out_sems.at[at]).wait()
        return carry

    lax.fori_loop(0, count, wait_block, 0)


def blocks(place, slot_of, source_ids, row_ids, tiles, scale_row, scale_got, sources, prior=None):
    local_rows, slots, side, _ = tiles.shape
    total, cands = source_ids.shape[0], place.shape[1]
    every = local_rows * cands
    extra = [] if prior is None else [prior]
    return pl.pallas_call(
        functools.partial(blocks_kernel, total, prior is not None),
        out_shape=jax.ShapeDtypeStruct((local_rows, cands, side, side), jnp.bfloat16),
        in_specs=[SMEM] * 4 + [VMEM] * 3 + [HBM] * (len(extra) + len(sources)),
        out_specs=HBM,
        input_output_aliases={7: 0} if extra else {},
        scratch_shapes=[
            pltpu.VMEM((total,) + tiles.shape[1:], tiles.dtype),
            pltpu.VMEM((local_rows, side, side), jnp.float32),
            pltpu.VMEM((every + every % 2, side, side), jnp.bfloat16),
            pltpu.SMEM((every,), jnp.int32),
            pltpu.SemaphoreType.DMA((total,)),
            pltpu.SemaphoreType.DMA((every,)),
        ],
        compiler_params=PARAMS,
        cost_estimate=pl.CostEstimate(
            flops=2 * total * every // 16 * slots * side**3, bytes_accessed=2 * (total + local_rows) * slots * side**2,
            transcendentals=0,
        ),
        name="blocks",
    )(
        place.reshape(-1), slot_of.reshape(-1), source_ids, row_ids, tiles, scale_row[:, None, :], scale_got[:, None, :],
        *extra, *sources,
    )


def exchange_direct(wanted_by, me, tiles):
    asked = lax.dynamic_index_in_dim(wanted_by, me, axis=1, keepdims=False)
    (send,) = pick_rows(asked, tiles, (asked.shape[0],))
    return lax.all_to_all(send, "col", split_axis=0, concat_axis=0, tiled=True)


def moves(targets, flip=0):
    return [(4 * z + p, 4 * t + (p ^ flip)) for z, t in enumerate(targets) if t is not None for p in range(4)]


PLANES = [[4 * z + p for p in range(4)] for z in range(4)]


def relay(wanted_by, me, tiles, middle):
    plane, mate = me // 4, me % 4
    inner = (plane == 1) | (plane == 2)
    flips = jnp.arange(4, dtype=jnp.int32)
    peer_ids = jnp.arange(16, dtype=jnp.int32)

    def lookup(readers, owner):
        of_owner = jnp.sum(jnp.where(peer_ids == owner, wanted_by, 0), axis=1)
        return jnp.sum(jnp.where(readers[:, None] == peer_ids, of_owner, 0), axis=1)

    beyond = 4 * (plane ^ 3) + (mate ^ flips)
    mine = lookup(jnp.concatenate([4 * (plane ^ 1) + flips, 4 * plane + flips, beyond[:1]]), me)
    (beside_send,) = pick_rows(mine[:4], tiles, (4,))
    beside = lax.ppermute(beside_send, "col", moves([1, 0, 3, 2]))
    own_send, first_send = pick_rows(mine[4:], tiles, (4, 1))
    own = lax.all_to_all(own_send, "col", split_axis=0, concat_axis=0, axis_index_groups=PLANES, tiled=True)
    near = lax.all_to_all(beside, "col", split_axis=0, concat_axis=0, axis_index_groups=PLANES, tiled=True)
    beyond_got = [lax.ppermute(first_send, "col", moves([3, None, None, 0]))]

    readers = jnp.concatenate(
        [jnp.where(inner, 4 * plane, 4 * (plane ^ 3)) + (mate ^ flips[1:]),
         jnp.where(inner, 4 * (plane ^ 1), 4 * (plane ^ 2)) + (mate ^ flips)]
    )
    rows = lookup(readers, jnp.where(inner, 4 * (plane ^ 3) + mate, me))
    sends = move_rows(jnp.where(inner, 1, 0) + 0 * rows, rows, (1,) * 7, tiles, middle)
    beyond_got += [lax.ppermute(sends[m - 1], "col", moves([3, 1, 2, 0], m)) for m in (1, 2, 3)]
    across_got = [lax.ppermute(sends[m + 3], "col", moves([2, 0, 3, 1], m)) for m in range(4)]

    near_owners = jnp.concatenate([4 * plane + flips, 4 * (plane ^ 1) + flips])
    across = 4 * (plane ^ 2) + (mate ^ flips)
    from_middle = inner & (flips == 0)
    two, none = flips[:2], 0 * flips
    return [
        (near_owners, jnp.concatenate([none, none + 1]), jnp.concatenate([flips, flips]), [own, near]),
        (
            jnp.concatenate([beyond, across[:2]]),
            jnp.concatenate([jnp.where(from_middle, 0, 1 + flips), 5 + two]),
            jnp.concatenate([jnp.where(from_middle, lookup(me[None], beyond[0]), 0), none[:2]]),
            [middle, *beyond_got, *across_got[:2]],
        ),
        (across[2:], two, none[:2], across_got[2:]),
    ]


def note_kernel(peers, candidates_ref, count_ref, cols_ref, degree_ref, out_ref):
    local_rows, cands = candidates_ref.shape
    side, slots = degree_ref.shape[1], cols_ref.shape[1]
    words = out_ref.shape[1] - local_rows
    lane = lax.broadcasted_iota(jnp.int32, (words, side), 0) * side
    lane = lane + lax.broadcasted_iota(jnp.int32, (words, side), 1)
    line = jnp.zeros_like(lane)
    for i in range(local_rows):
        for q in range(cands):
            candidate = candidates_ref[i, q]
            owner = candidate // local_rows
            line = jnp.where(lane == owner, candidate - owner * local_rows, line)
        line = jnp.where(lane == peers + i, count_ref[i], line)
        for r in range(slots):
            line = jnp.where(lane == peers + local_rows + i * slots + r, cols_ref[i, r], line)
    note = jnp.concatenate([degree_ref[...], line], axis=0)
    for peer in range(peers):
        out_ref[peer] = note


def write_note(candidates, tile_count, tile_cols, degree, peers):
    local_rows, side = degree.shape
    words = -(-(peers + local_rows + tile_cols.size) // side)
    return pl.pallas_call(
        functools.partial(note_kernel, peers),
        out_shape=jax.ShapeDtypeStruct((peers, local_rows + words, side), jnp.int32),
        in_specs=[SMEM, SMEM, SMEM, VMEM],
        out_specs=VMEM,
        name="write_note",
    )(candidates, tile_count, tile_cols, degree)


def local(tiles, tile_cols, tile_count, candidates, degree):
    local_rows, slots, side, _ = tiles.shape
    peers = lax.axis_size("col")
    me = lax.axis_index("col")
    owners = candidates // local_rows
    peer_ids = jnp.arange(peers, dtype=jnp.int32)
    row_ids = jnp.arange(local_rows, dtype=jnp.int32)

    matches = owners[:, :, None] == peer_ids
    note = write_note(candidates, tile_count, tile_cols, degree, peers)
    notes = lax.all_to_all(note, "col", split_axis=0, concat_axis=0, tiled=True)
    relayed = peers == 16
    if relayed:
        middle = lax.ppermute(tiles, "col", moves([None, 2, 1, None]))
    degree_all = notes[:, :local_rows]
    notes = notes[:, local_rows:].reshape(peers, -1)
    wanted = jnp.max(jnp.where(matches, (candidates % local_rows)[:, :, None], 0), axis=(0, 1))
    wanted_by = notes[:, :peers]
    at = peers
    counts_all = notes[:, at : at + local_rows]
    at += local_rows
    cols_all = notes[:, at : at + local_rows * slots].reshape(peers, local_rows, slots)

    mine = wanted[:, None] == row_ids
    count_got = jnp.sum(jnp.where(mine, counts_all, 0), axis=1)
    cols_got = jnp.sum(jnp.where(mine[:, :, None], cols_all, 0), axis=1)
    degree_got = jnp.sum(jnp.where(mine[:, :, None], degree_all, 0), axis=1)
    slot_ids = jnp.arange(slots, dtype=jnp.int32)
    cols_got = jnp.where(slot_ids < count_got[:, None], cols_got, -1)
    cols_other = jnp.sum(jnp.where(matches[..., None], cols_got, 0), axis=2)
    cols_mine = jnp.where(slot_ids < tile_count[:, None], tile_cols, -2)
    meets = cols_mine[:, None, :, None] == cols_other[:, :, None, :]
    slot_of = jnp.sum(jnp.where(meets, slot_ids + 1, 0), axis=3) - 1

    scale_row = lax.rsqrt(degree.astype(jnp.float32))
    scale_other = lax.rsqrt(degree_got.astype(jnp.float32))

    if relayed:
        parts = relay(wanted_by, me, tiles, middle)
    else:
        parts = [(peer_ids, jnp.zeros_like(peer_ids), peer_ids, [exchange_direct(wanted_by, me, tiles)])]
    done = None
    for owner_ids, source_ids, row_ids, sources in parts:
        at = jnp.arange(owner_ids.shape[0], dtype=jnp.int32)
        place = jnp.sum(jnp.where(owners[:, :, None] == owner_ids, at + 1, 0), axis=2) - 1
        scale_got = jnp.sum(jnp.where((owner_ids[:, None] == peer_ids)[:, :, None], scale_other, 0.0), axis=1)
        done = blocks(place, slot_of, source_ids, row_ids, tiles, scale_row, scale_got, sources, done)
    return done


def solution(mesh):
    in_specs = (
        P(("slab", "col"), None, None, None),
        P(("slab", "col"), None),
        P(("slab", "col")),
        P(("slab", "col"), None),
        P(("slab", "col"), None),
    )
    out_specs = P(("slab", "col"), None, None, None)
    return jax.shard_map(local, mesh=mesh, in_specs=in_specs, out_specs=out_specs, check_vma=False)
```

```python
import functools

import jax
import jax.numpy as jnp
from jax import lax
from jax.experimental import pallas as pl
from jax.experimental.pallas import tpu as pltpu
from jax.sharding import PartitionSpec as P

VMEM_LIMIT = 48 * 1024 * 1024
TOGETHER = 4
SMEM = pl.BlockSpec(memory_space=pltpu.SMEM)
VMEM = pl.BlockSpec(memory_space=pltpu.VMEM)
HBM = pl.BlockSpec(memory_space=pl.ANY)
PARAMS = pltpu.CompilerParams(vmem_limit_bytes=VMEM_LIMIT)
WHOLE_VMEM = pltpu.CompilerParams(vmem_limit_bytes=62 * 1024 * 1024)


def start_rows(total, source_ref, row_ref, sources, target_ref, sems):
    for k in range(total):
        for at, ref in enumerate(sources):
            last = at == len(sources) - 1

            @pl.when(source_ref[k] >= at if last else source_ref[k] == at)
            def _():
                pltpu.make_async_copy(ref.at[row_ref[k]], target_ref.at[k], sems.at[k]).start()


def wait_rows(total, sources, target_ref, sems):
    for k in range(total):
        pltpu.make_async_copy(sources[0].at[0], target_ref.at[k], sems.at[k]).wait()


def move_rows_kernel(sizes, source_ref, row_ref, *refs):
    *sources, stage_ref, sems, out_sems = refs
    sources, outs = sources[: -len(sizes)], sources[-len(sizes) :]
    places = [ref.at[k] for ref, size in zip(outs, sizes) for k in range(size)]
    start_rows(len(places), source_ref, row_ref, sources, stage_ref, sems)
    for k, place in enumerate(places):
        pltpu.make_async_copy(sources[0].at[0], stage_ref.at[k], sems.at[k]).wait()
        pltpu.make_async_copy(stage_ref.at[k], place, out_sems.at[k]).start()
    for k, place in enumerate(places):
        pltpu.make_async_copy(stage_ref.at[k], place, out_sems.at[k]).wait()


def move_rows(source_ids, row_ids, sizes, *sources):
    row, dtype = sources[0].shape[1:], sources[0].dtype
    return pl.pallas_call(
        functools.partial(move_rows_kernel, sizes),
        out_shape=[jax.ShapeDtypeStruct((size,) + row, dtype) for size in sizes],
        in_specs=[SMEM, SMEM] + [HBM] * len(sources),
        out_specs=[HBM] * len(sizes),
        scratch_shapes=[
            pltpu.VMEM((sum(sizes),) + row, dtype),
            pltpu.SemaphoreType.DMA((sum(sizes),)),
            pltpu.SemaphoreType.DMA((sum(sizes),)),
        ],
        compiler_params=WHOLE_VMEM,
        name="move_rows",
    )(source_ids, row_ids, *sources)


def pick_rows(rows, tiles, sizes):
    return move_rows(jnp.zeros_like(rows), rows, sizes, tiles)


def blocks_kernel(total, prior, place_ref, slot_ref, source_ref, row_ref, tiles_ref, scale_row_ref, scale_got_ref, *refs):
    *sources, out_ref, fetched_ref, scale_ref, stage_ref, list_ref, sems, out_sems = refs
    if prior:
        sources = sources[1:]
    local_rows, slots, side, _ = tiles_ref.shape
    cands = out_ref.shape[1]
    start_rows(total, source_ref, row_ref, sources, fetched_ref, sems)

    def note_block(block, count):
        place = place_ref[block]

        @pl.when(place >= 0)
        def _():
            list_ref[count] = block

        return count + (place >= 0).astype(jnp.int32)

    count = lax.fori_loop(0, local_rows * cands, note_block, jnp.int32(0))
    for i in range(local_rows):
        scale_ref[i] = jnp.broadcast_to(scale_row_ref[i], (side, side)).T
    wait_rows(total, sources, fetched_ref, sems)

    def some_blocks(step, carry):
        for k in range(TOGETHER):
            at = TOGETHER * step + k
            block = list_ref[jnp.minimum(at, count - 1)]
            i, place = block // cands, place_ref[block]
            left, right = [], []
            for r in range(slots):
                s = slot_ref[block * slots + r]
                tile = fetched_ref[place, jnp.maximum(s, 0)]
                right.append(jnp.where(s >= 0, tile, jnp.zeros_like(tile)))
                left.append(tiles_ref[i, r])
            shared = lax.dot_general(
                jnp.concatenate(left, axis=1), jnp.concatenate(right, axis=1), (((1,), (1,)), ((), ())),
                preferred_element_type=jnp.float32,
            )
            stage_ref[at] = (shared * (scale_ref[i] * scale_got_ref[place])).astype(stage_ref.dtype)
        for k in range(TOGETHER):
            at = TOGETHER * step + k

            @pl.when(at < count)
            def _():
                block = list_ref[at]
                to = out_ref.at[block // cands, lax.rem(block, cands)]
                pltpu.make_async_copy(stage_ref.at[at], to, out_sems.at[at]).start()

        return carry

    lax.fori_loop(0, (count + TOGETHER - 1) // TOGETHER, some_blocks, 0)

    def wait_block(at, carry):
        pltpu.make_async_copy(stage_ref.at[at], out_ref.at[0, 0], out_sems.at[at]).wait()
        return carry

    lax.fori_loop(0, count, wait_block, 0)


def blocks(place, slot_of, source_ids, row_ids, tiles, scale_row, scale_got, sources, prior=None):
    local_rows, slots, side, _ = tiles.shape
    total, cands = source_ids.shape[0], place.shape[1]
    every = local_rows * cands
    extra = [] if prior is None else [prior]
    return pl.pallas_call(
        functools.partial(blocks_kernel, total, prior is not None),
        out_shape=jax.ShapeDtypeStruct((local_rows, cands, side, side), jnp.bfloat16),
        in_specs=[SMEM] * 4 + [VMEM] * 3 + [HBM] * (len(extra) + len(sources)),
        out_specs=HBM,
        input_output_aliases={7: 0} if extra else {},
        scratch_shapes=[
            pltpu.VMEM((total,) + tiles.shape[1:], tiles.dtype),
            pltpu.VMEM((local_rows, side, side), jnp.float32),
            pltpu.VMEM((every + -every % TOGETHER, side, side), jnp.bfloat16),
            pltpu.SMEM((every,), jnp.int32),
            pltpu.SemaphoreType.DMA((total,)),
            pltpu.SemaphoreType.DMA((every,)),
        ],
        compiler_params=PARAMS,
        cost_estimate=pl.CostEstimate(
            flops=2 * total * every // 16 * slots * side**3, bytes_accessed=2 * (total + local_rows) * slots * side**2,
            transcendentals=0,
        ),
        name="blocks",
    )(
        place.reshape(-1), slot_of.reshape(-1), source_ids, row_ids, tiles, scale_row[:, None, :], scale_got[:, None, :],
        *extra, *sources,
    )


def exchange_direct(wanted_by, me, tiles):
    asked = lax.dynamic_index_in_dim(wanted_by, me, axis=1, keepdims=False)
    (send,) = pick_rows(asked, tiles, (asked.shape[0],))
    return lax.all_to_all(send, "col", split_axis=0, concat_axis=0, tiled=True)


def moves(targets, flip=0):
    return [(4 * z + p, 4 * t + (p ^ flip)) for z, t in enumerate(targets) if t is not None for p in range(4)]


PLANES = [[4 * z + p for p in range(4)] for z in range(4)]


def relay(wanted_by, me, tiles, middle):
    plane, mate = me // 4, me % 4
    inner = (plane == 1) | (plane == 2)
    flips = jnp.arange(4, dtype=jnp.int32)
    peer_ids = jnp.arange(16, dtype=jnp.int32)

    def lookup(readers, owner):
        of_owner = jnp.sum(jnp.where(peer_ids == owner, wanted_by, 0), axis=1)
        return jnp.sum(jnp.where(readers[:, None] == peer_ids, of_owner, 0), axis=1)

    beyond = 4 * (plane ^ 3) + (mate ^ flips)
    mine = lookup(jnp.concatenate([4 * (plane ^ 1) + flips, 4 * plane + flips, beyond[:1]]), me)
    (beside_send,) = pick_rows(mine[:4], tiles, (4,))
    beside = lax.ppermute(beside_send, "col", moves([1, 0, 3, 2]))
    own_send, first_send = pick_rows(mine[4:], tiles, (4, 1))
    own = lax.all_to_all(own_send, "col", split_axis=0, concat_axis=0, axis_index_groups=PLANES, tiled=True)
    near = lax.all_to_all(beside, "col", split_axis=0, concat_axis=0, axis_index_groups=PLANES, tiled=True)
    beyond_got = [lax.ppermute(first_send, "col", moves([3, None, None, 0]))]

    readers = jnp.concatenate(
        [jnp.where(inner, 4 * plane, 4 * (plane ^ 3)) + (mate ^ flips[1:]),
         jnp.where(inner, 4 * (plane ^ 1), 4 * (plane ^ 2)) + (mate ^ flips)]
    )
    rows = lookup(readers, jnp.where(inner, 4 * (plane ^ 3) + mate, me))
    sends = move_rows(jnp.where(inner, 1, 0) + 0 * rows, rows, (1,) * 7, tiles, middle)
    beyond_got += [lax.ppermute(sends[m - 1], "col", moves([3, 1, 2, 0], m)) for m in (1, 2, 3)]
    across_got = [lax.ppermute(sends[m + 3], "col", moves([2, 0, 3, 1], m)) for m in range(4)]

    near_owners = jnp.concatenate([4 * plane + flips, 4 * (plane ^ 1) + flips])
    across = 4 * (plane ^ 2) + (mate ^ flips)
    from_middle = inner & (flips == 0)
    two, none = flips[:2], 0 * flips
    return [
        (near_owners, jnp.concatenate([none, none + 1]), jnp.concatenate([flips, flips]), [own, near]),
        (
            jnp.concatenate([beyond, across[:2]]),
            jnp.concatenate([jnp.where(from_middle, 0, 1 + flips), 5 + two]),
            jnp.concatenate([jnp.where(from_middle, lookup(me[None], beyond[0]), 0), none[:2]]),
            [middle, *beyond_got, *across_got[:2]],
        ),
        (across[2:], two, none[:2], across_got[2:]),
    ]


def note_kernel(peers, candidates_ref, count_ref, cols_ref, degree_ref, out_ref):
    local_rows, cands = candidates_ref.shape
    side, slots = degree_ref.shape[1], cols_ref.shape[1]
    words = out_ref.shape[1] - local_rows
    lane = lax.broadcasted_iota(jnp.int32, (words, side), 0) * side
    lane = lane + lax.broadcasted_iota(jnp.int32, (words, side), 1)
    line = jnp.zeros_like(lane)
    for i in range(local_rows):
        for q in range(cands):
            candidate = candidates_ref[i, q]
            owner = candidate // local_rows
            line = jnp.where(lane == owner, candidate - owner * local_rows, line)
        line = jnp.where(lane == peers + i, count_ref[i], line)
        for r in range(slots):
            line = jnp.where(lane == peers + local_rows + i * slots + r, cols_ref[i, r], line)
    note = jnp.concatenate([degree_ref[...], line], axis=0)
    for peer in range(peers):
        out_ref[peer] = note


def write_note(candidates, tile_count, tile_cols, degree, peers):
    local_rows, side = degree.shape
    words = -(-(peers + local_rows + tile_cols.size) // side)
    return pl.pallas_call(
        functools.partial(note_kernel, peers),
        out_shape=jax.ShapeDtypeStruct((peers, local_rows + words, side), jnp.int32),
        in_specs=[SMEM, SMEM, SMEM, VMEM],
        out_specs=VMEM,
        name="write_note",
    )(candidates, tile_count, tile_cols, degree)


def local(tiles, tile_cols, tile_count, candidates, degree):
    local_rows, slots, side, _ = tiles.shape
    peers = lax.axis_size("col")
    me = lax.axis_index("col")
    owners = candidates // local_rows
    peer_ids = jnp.arange(peers, dtype=jnp.int32)
    row_ids = jnp.arange(local_rows, dtype=jnp.int32)

    matches = owners[:, :, None] == peer_ids
    note = write_note(candidates, tile_count, tile_cols, degree, peers)
    notes = lax.all_to_all(note, "col", split_axis=0, concat_axis=0, tiled=True)
    relayed = peers == 16
    if relayed:
        middle = lax.ppermute(tiles, "col", moves([None, 2, 1, None]))
    degree_all = notes[:, :local_rows]
    notes = notes[:, local_rows:].reshape(peers, -1)
    wanted = jnp.max(jnp.where(matches, (candidates % local_rows)[:, :, None], 0), axis=(0, 1))
    wanted_by = notes[:, :peers]
    at = peers
    counts_all = notes[:, at : at + local_rows]
    at += local_rows
    cols_all = notes[:, at : at + local_rows * slots].reshape(peers, local_rows, slots)

    mine = wanted[:, None] == row_ids
    count_got = jnp.sum(jnp.where(mine, counts_all, 0), axis=1)
    cols_got = jnp.sum(jnp.where(mine[:, :, None], cols_all, 0), axis=1)
    degree_got = jnp.sum(jnp.where(mine[:, :, None], degree_all, 0), axis=1)
    slot_ids = jnp.arange(slots, dtype=jnp.int32)
    cols_got = jnp.where(slot_ids < count_got[:, None], cols_got, -1)
    cols_other = jnp.sum(jnp.where(matches[..., None], cols_got, 0), axis=2)
    cols_mine = jnp.where(slot_ids < tile_count[:, None], tile_cols, -2)
    meets = cols_mine[:, None, :, None] == cols_other[:, :, None, :]
    slot_of = jnp.sum(jnp.where(meets, slot_ids + 1, 0), axis=3) - 1

    scale_row = lax.rsqrt(degree.astype(jnp.float32))
    scale_other = lax.rsqrt(degree_got.astype(jnp.float32))

    if relayed:
        parts = relay(wanted_by, me, tiles, middle)
    else:
        parts = [(peer_ids, jnp.zeros_like(peer_ids), peer_ids, [exchange_direct(wanted_by, me, tiles)])]
    done = None
    for owner_ids, source_ids, row_ids, sources in parts:
        at = jnp.arange(owner_ids.shape[0], dtype=jnp.int32)
        place = jnp.sum(jnp.where(owners[:, :, None] == owner_ids, at + 1, 0), axis=2) - 1
        scale_got = jnp.sum(jnp.where((owner_ids[:, None] == peer_ids)[:, :, None], scale_other, 0.0), axis=1)
        done = blocks(place, slot_of, source_ids, row_ids, tiles, scale_row, scale_got, sources, done)
    return done


def solution(mesh):
    in_specs = (
        P(("slab", "col"), None, None, None),
        P(("slab", "col"), None),
        P(("slab", "col")),
        P(("slab", "col"), None),
        P(("slab", "col"), None),
    )
    out_specs = P(("slab", "col"), None, None, None)
    return jax.shard_map(local, mesh=mesh, in_specs=in_specs, out_specs=out_specs, check_vma=False)
```

```python
import functools

import jax
import jax.numpy as jnp
from jax import lax
from jax.experimental import pallas as pl
from jax.experimental.pallas import tpu as pltpu
from jax.sharding import PartitionSpec as P

VMEM_LIMIT = 48 * 1024 * 1024
SMEM = pl.BlockSpec(memory_space=pltpu.SMEM)
VMEM = pl.BlockSpec(memory_space=pltpu.VMEM)
HBM = pl.BlockSpec(memory_space=pl.ANY)
PARAMS = pltpu.CompilerParams(vmem_limit_bytes=VMEM_LIMIT)
WHOLE_VMEM = pltpu.CompilerParams(vmem_limit_bytes=62 * 1024 * 1024)


def start_rows(total, source_ref, row_ref, sources, target_ref, sems):
    for k in range(total):
        for at, ref in enumerate(sources):
            last = at == len(sources) - 1

            @pl.when(source_ref[k] >= at if last else source_ref[k] == at)
            def _():
                pltpu.make_async_copy(ref.at[row_ref[k]], target_ref.at[k], sems.at[k]).start()


def wait_rows(total, sources, target_ref, sems):
    for k in range(total):
        pltpu.make_async_copy(sources[0].at[0], target_ref.at[k], sems.at[k]).wait()


def move_rows_kernel(sizes, source_ref, row_ref, *refs):
    *sources, stage_ref, sems, out_sems = refs
    sources, outs = sources[: -len(sizes)], sources[-len(sizes) :]
    places = [ref.at[k] for ref, size in zip(outs, sizes) for k in range(size)]
    start_rows(len(places), source_ref, row_ref, sources, stage_ref, sems)
    for k, place in enumerate(places):
        pltpu.make_async_copy(sources[0].at[0], stage_ref.at[k], sems.at[k]).wait()
        pltpu.make_async_copy(stage_ref.at[k], place, out_sems.at[k]).start()
    for k, place in enumerate(places):
        pltpu.make_async_copy(stage_ref.at[k], place, out_sems.at[k]).wait()


def move_rows(source_ids, row_ids, sizes, *sources):
    row, dtype = sources[0].shape[1:], sources[0].dtype
    return pl.pallas_call(
        functools.partial(move_rows_kernel, sizes),
        out_shape=[jax.ShapeDtypeStruct((size,) + row, dtype) for size in sizes],
        in_specs=[SMEM, SMEM] + [HBM] * len(sources),
        out_specs=[HBM] * len(sizes),
        scratch_shapes=[
            pltpu.VMEM((sum(sizes),) + row, dtype),
            pltpu.SemaphoreType.DMA((sum(sizes),)),
            pltpu.SemaphoreType.DMA((sum(sizes),)),
        ],
        compiler_params=WHOLE_VMEM,
        name="move_rows",
    )(source_ids, row_ids, *sources)


def stack_kernel(row_ref, tiles_ref, out_ref, sems):
    for k in range(out_ref.shape[0]):
        pltpu.make_async_copy(tiles_ref.at[row_ref[k]], out_ref.at[k], sems.at[k]).start()
    for k in range(out_ref.shape[0]):
        pltpu.make_async_copy(tiles_ref.at[0], out_ref.at[k], sems.at[k]).wait()


def stack_rows(rows, tiles):
    return pl.pallas_call(
        stack_kernel,
        out_shape=jax.ShapeDtypeStruct(rows.shape + tiles.shape[1:], tiles.dtype),
        in_specs=[SMEM, HBM],
        out_specs=VMEM,
        scratch_shapes=[pltpu.SemaphoreType.DMA(rows.shape)],
        compiler_params=PARAMS,
        name="stack_rows",
    )(rows, tiles)


def pick_rows(rows, tiles, sizes):
    return move_rows(jnp.zeros_like(rows), rows, sizes, tiles)


def blocks_kernel(total, prior, place_ref, slot_ref, source_ref, row_ref, tiles_ref, scale_row_ref, scale_got_ref, *refs):
    *sources, out_ref, fetched_ref, scale_ref, stage_ref, list_ref, sems, out_sems = refs
    if prior:
        sources = sources[1:]
    local_rows, slots, side, _ = tiles_ref.shape
    cands = out_ref.shape[1]
    start_rows(total, source_ref, row_ref, sources, fetched_ref, sems)

    def note_block(block, count):
        place = place_ref[block]

        @pl.when(place >= 0)
        def _():
            list_ref[count] = block

        return count + (place >= 0).astype(jnp.int32)

    count = lax.fori_loop(0, local_rows * cands, note_block, jnp.int32(0))
    for i in range(local_rows):
        scale_ref[i] = jnp.broadcast_to(scale_row_ref[i], (side, side)).T
    wait_rows(total, sources, fetched_ref, sems)

    def two_blocks(step, carry):
        for k in (0, 1):
            at = 2 * step + k
            block = list_ref[jnp.minimum(at, count - 1)]
            i, place = block // cands, place_ref[block]
            left, right = [], []
            for r in range(slots):
                s = slot_ref[block * slots + r]
                tile = fetched_ref[place, jnp.maximum(s, 0)]
                right.append(jnp.where(s >= 0, tile, jnp.zeros_like(tile)))
                left.append(tiles_ref[i, r])
            shared = lax.dot_general(
                jnp.concatenate(left, axis=1), jnp.concatenate(right, axis=1), (((1,), (1,)), ((), ())),
                preferred_element_type=jnp.float32,
            )
            stage_ref[at] = (shared * (scale_ref[i] * scale_got_ref[place])).astype(stage_ref.dtype)
        for k in (0, 1):
            at = 2 * step + k

            @pl.when(at < count)
            def _():
                block = list_ref[at]
                to = out_ref.at[block // cands, lax.rem(block, cands)]
                pltpu.make_async_copy(stage_ref.at[at], to, out_sems.at[at]).start()

        return carry

    lax.fori_loop(0, (count + 1) // 2, two_blocks, 0)

    def wait_block(at, carry):
        pltpu.make_async_copy(stage_ref.at[at], out_ref.at[0, 0], out_sems.at[at]).wait()
        return carry

    lax.fori_loop(0, count, wait_block, 0)


def blocks(place, slot_of, source_ids, row_ids, tiles, scale_row, scale_got, sources, prior=None):
    local_rows, slots, side, _ = tiles.shape
    total, cands = source_ids.shape[0], place.shape[1]
    every = local_rows * cands
    extra = [] if prior is None else [prior]
    return pl.pallas_call(
        functools.partial(blocks_kernel, total, prior is not None),
        out_shape=jax.ShapeDtypeStruct((local_rows, cands, side, side), jnp.bfloat16),
        in_specs=[SMEM] * 4 + [VMEM] * 3 + [HBM] * (len(extra) + len(sources)),
        out_specs=HBM,
        input_output_aliases={7: 0} if extra else {},
        scratch_shapes=[
            pltpu.VMEM((total,) + tiles.shape[1:], tiles.dtype),
            pltpu.VMEM((local_rows, side, side), jnp.float32),
            pltpu.VMEM((every + every % 2, side, side), jnp.bfloat16),
            pltpu.SMEM((every,), jnp.int32),
            pltpu.SemaphoreType.DMA((total,)),
            pltpu.SemaphoreType.DMA((every,)),
        ],
        compiler_params=PARAMS,
        cost_estimate=pl.CostEstimate(
            flops=2 * total * every // 16 * slots * side**3, bytes_accessed=2 * (total + local_rows) * slots * side**2,
            transcendentals=0,
        ),
        name="blocks",
    )(
        place.reshape(-1), slot_of.reshape(-1), source_ids, row_ids, tiles, scale_row[:, None, :], scale_got[:, None, :],
        *extra, *sources,
    )


def exchange_direct(wanted_by, me, tiles):
    asked = lax.dynamic_index_in_dim(wanted_by, me, axis=1, keepdims=False)
    (send,) = pick_rows(asked, tiles, (asked.shape[0],))
    return lax.all_to_all(send, "col", split_axis=0, concat_axis=0, tiled=True)


def moves(targets, flip=0):
    return [(4 * z + p, 4 * t + (p ^ flip)) for z, t in enumerate(targets) if t is not None for p in range(4)]


PLANES = [[4 * z + p for p in range(4)] for z in range(4)]


def relay(wanted_by, me, tiles, middle):
    plane, mate = me // 4, me % 4
    inner = (plane == 1) | (plane == 2)
    flips = jnp.arange(4, dtype=jnp.int32)
    peer_ids = jnp.arange(16, dtype=jnp.int32)

    def lookup(readers, owner):
        of_owner = jnp.sum(jnp.where(peer_ids == owner, wanted_by, 0), axis=1)
        return jnp.sum(jnp.where(readers[:, None] == peer_ids, of_owner, 0), axis=1)

    beyond = 4 * (plane ^ 3) + (mate ^ flips)
    mine = lookup(jnp.concatenate([4 * (plane ^ 1) + flips, 4 * plane + flips, beyond[:1]]), me)
    beside_send = stack_rows(mine[:4], tiles)
    beside = lax.ppermute(beside_send, "col", moves([1, 0, 3, 2]))
    own_send, first_send = pick_rows(mine[4:], tiles, (4, 1))
    own = lax.all_to_all(own_send, "col", split_axis=0, concat_axis=0, axis_index_groups=PLANES, tiled=True)
    near = lax.all_to_all(beside, "col", split_axis=0, concat_axis=0, axis_index_groups=PLANES, tiled=True)
    beyond_got = [lax.ppermute(first_send, "col", moves([3, None, None, 0]))]

    readers = jnp.concatenate(
        [jnp.where(inner, 4 * plane, 4 * (plane ^ 3)) + (mate ^ flips[1:]),
         jnp.where(inner, 4 * (plane ^ 1), 4 * (plane ^ 2)) + (mate ^ flips)]
    )
    rows = lookup(readers, jnp.where(inner, 4 * (plane ^ 3) + mate, me))
    sends = move_rows(jnp.where(inner, 1, 0) + 0 * rows, rows, (1,) * 7, tiles, middle)
    beyond_got += [lax.ppermute(sends[m - 1], "col", moves([3, 1, 2, 0], m)) for m in (1, 2, 3)]
    across_got = [lax.ppermute(sends[m + 3], "col", moves([2, 0, 3, 1], m)) for m in range(4)]

    near_owners = jnp.concatenate([4 * plane + flips, 4 * (plane ^ 1) + flips])
    across = 4 * (plane ^ 2) + (mate ^ flips)
    from_middle = inner & (flips == 0)
    two, none = flips[:2], 0 * flips
    return [
        (near_owners, jnp.concatenate([none, none + 1]), jnp.concatenate([flips, flips]), [own, near]),
        (
            jnp.concatenate([beyond, across[:2]]),
            jnp.concatenate([jnp.where(from_middle, 0, 1 + flips), 5 + two]),
            jnp.concatenate([jnp.where(from_middle, lookup(me[None], beyond[0]), 0), none[:2]]),
            [middle, *beyond_got, *across_got[:2]],
        ),
        (across[2:], two, none[:2], across_got[2:]),
    ]


def note_kernel(peers, candidates_ref, count_ref, cols_ref, degree_ref, out_ref):
    local_rows, cands = candidates_ref.shape
    side, slots = degree_ref.shape[1], cols_ref.shape[1]
    words = out_ref.shape[1] - local_rows
    lane = lax.broadcasted_iota(jnp.int32, (words, side), 0) * side
    lane = lane + lax.broadcasted_iota(jnp.int32, (words, side), 1)
    line = jnp.zeros_like(lane)
    for i in range(local_rows):
        for q in range(cands):
            candidate = candidates_ref[i, q]
            owner = candidate // local_rows
            line = jnp.where(lane == owner, candidate - owner * local_rows, line)
        line = jnp.where(lane == peers + i, count_ref[i], line)
        for r in range(slots):
            line = jnp.where(lane == peers + local_rows + i * slots + r, cols_ref[i, r], line)
    note = jnp.concatenate([degree_ref[...], line], axis=0)
    for peer in range(peers):
        out_ref[peer] = note


def write_note(candidates, tile_count, tile_cols, degree, peers):
    local_rows, side = degree.shape
    words = -(-(peers + local_rows + tile_cols.size) // side)
    return pl.pallas_call(
        functools.partial(note_kernel, peers),
        out_shape=jax.ShapeDtypeStruct((peers, local_rows + words, side), jnp.int32),
        in_specs=[SMEM, SMEM, SMEM, VMEM],
        out_specs=VMEM,
        name="write_note",
    )(candidates, tile_count, tile_cols, degree)


def local(tiles, tile_cols, tile_count, candidates, degree):
    local_rows, slots, side, _ = tiles.shape
    peers = lax.axis_size("col")
    me = lax.axis_index("col")
    owners = candidates // local_rows
    peer_ids = jnp.arange(peers, dtype=jnp.int32)
    row_ids = jnp.arange(local_rows, dtype=jnp.int32)

    matches = owners[:, :, None] == peer_ids
    note = write_note(candidates, tile_count, tile_cols, degree, peers)
    notes = lax.all_to_all(note, "col", split_axis=0, concat_axis=0, tiled=True)
    relayed = peers == 16
    if relayed:
        middle = lax.ppermute(tiles, "col", moves([None, 2, 1, None]))
    degree_all = notes[:, :local_rows]
    notes = notes[:, local_rows:].reshape(peers, -1)
    wanted = jnp.max(jnp.where(matches, (candidates % local_rows)[:, :, None], 0), axis=(0, 1))
    wanted_by = notes[:, :peers]
    at = peers
    counts_all = notes[:, at : at + local_rows]
    at += local_rows
    cols_all = notes[:, at : at + local_rows * slots].reshape(peers, local_rows, slots)

    mine = wanted[:, None] == row_ids
    count_got = jnp.sum(jnp.where(mine, counts_all, 0), axis=1)
    cols_got = jnp.sum(jnp.where(mine[:, :, None], cols_all, 0), axis=1)
    degree_got = jnp.sum(jnp.where(mine[:, :, None], degree_all, 0), axis=1)
    slot_ids = jnp.arange(slots, dtype=jnp.int32)
    cols_got = jnp.where(slot_ids < count_got[:, None], cols_got, -1)
    cols_other = jnp.sum(jnp.where(matches[..., None], cols_got, 0), axis=2)
    cols_mine = jnp.where(slot_ids < tile_count[:, None], tile_cols, -2)
    meets = cols_mine[:, None, :, None] == cols_other[:, :, None, :]
    slot_of = jnp.sum(jnp.where(meets, slot_ids + 1, 0), axis=3) - 1

    scale_row = lax.rsqrt(degree.astype(jnp.float32))
    scale_other = lax.rsqrt(degree_got.astype(jnp.float32))

    if relayed:
        parts = relay(wanted_by, me, tiles, middle)
    else:
        parts = [(peer_ids, jnp.zeros_like(peer_ids), peer_ids, [exchange_direct(wanted_by, me, tiles)])]
    done = None
    for owner_ids, source_ids, row_ids, sources in parts:
        at = jnp.arange(owner_ids.shape[0], dtype=jnp.int32)
        place = jnp.sum(jnp.where(owners[:, :, None] == owner_ids, at + 1, 0), axis=2) - 1
        scale_got = jnp.sum(jnp.where((owner_ids[:, None] == peer_ids)[:, :, None], scale_other, 0.0), axis=1)
        done = blocks(place, slot_of, source_ids, row_ids, tiles, scale_row, scale_got, sources, done)
    return done


def solution(mesh):
    in_specs = (
        P(("slab", "col"), None, None, None),
        P(("slab", "col"), None),
        P(("slab", "col")),
        P(("slab", "col"), None),
        P(("slab", "col"), None),
    )
    out_specs = P(("slab", "col"), None, None, None)
    return jax.shard_map(local, mesh=mesh, in_specs=in_specs, out_specs=out_specs, check_vma=False)
```
